32 devices in a mesh: rows: 8 (over y, x, core), rep: 4 (over z).
Axes of the slice: x: 2, y: 2, z: 4, core: 2. Of those that a mesh axis runs over, the one named last changes fastest.
Arguments:
- features: bfloat16 [4096, 256], P(('rows', 'rep')), may hold values from -6 to 6
- weight: bfloat16 [256, 256], replicated, may hold values from -0.375 to 0.375
- tiles: bfloat16 [8, 4, 4, 8, 128, 128], P('rows', 'rep'), as said below
- send_src: int32 [8, 4, 8, 24], P('rows', 'rep'), may hold values from 0 to 4095, as said below
- send_dst: int32 [8, 4, 8, 24], P('rows', 'rep'), may hold values from 0 to 128, as said below
- cotangent: bfloat16 [4096, 256], P(('rows', 'rep')), may hold values from -6 to 6
Outputs:
- output: bfloat16 [4096, 256], P(('rows', 'rep'))
- grad_w: float32 [256, 256], replicated
- grad_x: bfloat16 [4096, 256], P(('rows', 'rep'))
The draws below stay inside these ranges and needn't reach their ends.
Inputs may be any that keep to these rules, and one draw needn't show every extreme that they name: Device (g, c)'s tiles are nonnegative; a tile row is nonzero only if some live slot of that device names it. `send_src`: A flattened tile row (b * 8 + k) * 128 + i of the sending device. Each tile row is named by at most one live slot, and all live slots naming rows of one tile belong to one peer p. An empty slot holds 0. `send_dst`: 128 marks an empty slot. For each rep index c there is a peer p to which every device (g, c) sends all 24 slots live, and some device has an empty slot. Destination rows may repeat.
All inputs are finite; a program needn't handle non-finite values.
Results may differ from the reference program's by a relative error of at most 0.02.
Values may be sent and summed in bfloat16 or wider, within the bound.
No kernel may reach another device: no remote copies, remote signals or barrier semaphores. Data moves between devices by JAX's collectives and lax.ppermute only.
A program may use at most 64 MiB of HBM per device.

```python
import math
import jax
import jax.numpy as jnp
from jax import lax

F = 256
BLK = 128
ROWS_DEV = 128
KPC = 8
SLOTS = 24
GROUPS = 8
REPS = 4
CBLK = 4
NODES = 4096


def layout(key):
    base_key = jax.random.fold_in(key, 11)
    sub_keys = jax.random.split(base_key, 10)
    device_count = GROUPS * REPS
    tile_count = CBLK * KPC
    column_peer = jax.random.randint(sub_keys[0], (REPS,), 0, GROUPS)
    full_peer = jnp.tile(column_peer, GROUPS)
    first_draw = jax.random.randint(sub_keys[1], (device_count, tile_count), 0, GROUPS)
    second_draw = jax.random.randint(sub_keys[2], (device_count, tile_count), 0, GROUPS)
    offsets = jax.random.randint(sub_keys[3], (device_count, 1), 0, GROUPS)
    peers = (first_draw * second_draw // GROUPS + offsets) % GROUPS
    special = jax.random.randint(sub_keys[4], (device_count, 1), 0, tile_count)
    tile_index = jnp.arange(tile_count, dtype=jnp.int32)
    peers = jnp.where(tile_index[None, :] == special, full_peer[:, None], peers)
    matching = peers[:, :, None] == peers[:, None, :]
    earlier = tile_index[None, None, :] < tile_index[None, :, None]
    ranks = jnp.sum(matching & earlier, axis=2).astype(jnp.int32)
    peer_index = jnp.arange(GROUPS, dtype=jnp.int32)
    owned = peers[:, None, :] == peer_index[None, :, None]
    tally = jnp.sum(owned, axis=2).astype(jnp.int32)
    slot_index = jnp.arange(SLOTS, dtype=jnp.int32)
    divisor = jnp.maximum(tally, 1)[:, :, None]
    want_rank = slot_index[None, None, :] % divisor
    depth = slot_index[None, None, :] // divisor
    chosen = owned[:, :, None, :] & (ranks[:, None, None, :] == want_rank[:, :, :, None])
    tile_pick = jnp.sum(jnp.where(chosen, tile_index, 0), axis=3).astype(jnp.int32)
    row_start = jax.random.randint(sub_keys[5], (device_count, tile_count), 0, BLK)
    row_step = 2 * jax.random.randint(sub_keys[6], (device_count, tile_count), 0, BLK // 2) + 1
    flat_pick = tile_pick.reshape(device_count, GROUPS * SLOTS)
    start_sel = jnp.take_along_axis(row_start, flat_pick, axis=1).reshape(device_count, GROUPS, SLOTS)
    step_sel = jnp.take_along_axis(row_step, flat_pick, axis=1).reshape(device_count, GROUPS, SLOTS)
    row_pick = (start_sel + depth * step_sel) % BLK
    keeping = jax.random.randint(sub_keys[7], (device_count, GROUPS, SLOTS), 0, 8) > 0
    is_full = peer_index[None, :, None] == full_peer[:, None, None]
    live = (tally[:, :, None] > 0) & (keeping | is_full)
    blank_device = jax.random.randint(sub_keys[8], (), 0, device_count)
    device_index = jnp.arange(device_count, dtype=jnp.int32)
    blank_peer = (full_peer[:, None, None] + 1) % GROUPS
    blank = (device_index[:, None, None] == blank_device) & (peer_index[None, :, None] == blank_peer) & (slot_index[None, None, :] == SLOTS - 1)
    live = live & jnp.logical_not(blank)
    sources = jnp.where(live, tile_pick * BLK + row_pick, 0).astype(jnp.int32)
    landing_rows = jax.random.randint(sub_keys[9], (device_count, GROUPS, SLOTS), 0, ROWS_DEV)
    targets = jnp.where(live, landing_rows, ROWS_DEV).astype(jnp.int32)
    return (live, sources, targets)


def draw_send_src(key, part):
    live, sources, targets = layout(key)
    return sources.reshape(GROUPS, REPS, GROUPS, SLOTS)


def draw_send_dst(key, part):
    live, sources, targets = layout(key)
    return targets.reshape(GROUPS, REPS, GROUPS, SLOTS)


def draw_tiles(key, part):
    live, sources, targets = layout(key)
    device_count = GROUPS * REPS
    tile_count = CBLK * KPC
    device_index = jnp.broadcast_to(jnp.arange(device_count, dtype=jnp.int32)[:, None, None], sources.shape)
    marks = jnp.zeros((device_count, tile_count * BLK), jnp.float32)
    marks = marks.at[device_index, sources].max(live.astype(jnp.float32))
    value_key = jax.random.fold_in(key, 29)
    shape = (device_count, tile_count, BLK, BLK)
    values = jnp.exp(jax.random.uniform(value_key, shape, jnp.float32, math.log(0.05), 0.0))
    values = values * (1.5 / math.sqrt(BLK)) * marks.reshape(device_count, tile_count, BLK, 1)
    return values.reshape(GROUPS, REPS, CBLK, KPC, BLK, BLK).astype(jnp.bfloat16)


def level_of(rng, dims, pieces, least, largest):
    def one(axis_at, blocks):
        steps = jax.random.uniform(jax.random.fold_in(jax.random.fold_in(rng, 6), axis_at), (blocks,), jnp.float32, least / len(pieces), largest / len(pieces))
        return jnp.repeat(jnp.exp(steps), dims[axis_at] // blocks).reshape((-1,) + (1,) * (len(dims) - axis_at - 1))

    level = one(*pieces[0])
    for cut in pieces[1:]:
        level = level * one(*cut)
    return level


def scatter_about(own_key, shape, scale, most, shards=(), held_as=jnp.bfloat16):
    entries = scale * jax.random.normal(own_key, shape, jnp.float32)
    if shards:
        entries = entries * level_of(own_key, shape, shards, -0.22, 0.18)
    return jnp.clip(entries, -most, most).astype(held_as)


def setup_inputs(seed: int = 0) -> dict:
    streams_of = jax.random.split(jax.random.key(seed), 7)
    features = scatter_about(streams_of[0], (NODES, F), 1.0, 6.0, ((0, 32),))
    weight = scatter_about(streams_of[1], (F, F), F ** -0.5, 0.375)
    tiles = draw_tiles(jax.random.fold_in(streams_of[6], 71), 0)
    send_src = draw_send_src(jax.random.fold_in(streams_of[6], 71), 0)
    send_dst = draw_send_dst(jax.random.fold_in(streams_of[6], 71), 0)
    cotangent = scatter_about(streams_of[5], (NODES, F), 1.0, 6.0, ((0, 32),))
    return dict(features=features, weight=weight, tiles=tiles, send_src=send_src, send_dst=send_dst, cotangent=cotangent)


def pick_rows(partial_rows, row_index):
    return partial_rows[row_index]

def place_rows(row_index, row_values, tile_rows, feature_width):
    return jnp.zeros((tile_rows, feature_width), jnp.float32).at[row_index].set(row_values.astype(jnp.float32), mode='drop')

def reference(features, weight, tiles, send_src, send_dst, cotangent):
    feature_width = features.shape[1]
    group_size = REPS * ROWS_DEV
    tile_rows = CBLK * KPC * BLK
    grouped = features.reshape(GROUPS, CBLK, BLK, feature_width)
    rep_index = jnp.arange(REPS, dtype=jnp.int32)
    peer_index = jnp.arange(GROUPS, dtype=jnp.int32)
    group_list = jnp.arange(GROUPS, dtype=jnp.int32)

    def destinations(group_dst):
        base_row = (peer_index[None, :, None] * REPS + rep_index[:, None, None]) * ROWS_DEV
        return jnp.where(group_dst < ROWS_DEV, base_row + group_dst, NODES).astype(jnp.int32)

    def forward_group(running, group_index):
        feature_blocks = grouped[group_index].astype(jnp.float32)
        tile_group = tiles[group_index].astype(jnp.float32)
        partial_value = jnp.einsum('cbkij,bjf->cbkif', tile_group, feature_blocks).reshape(REPS, tile_rows, feature_width)
        sources = send_src[group_index].reshape(REPS, GROUPS * SLOTS)
        fetched = jax.vmap(pick_rows)(partial_value, sources)
        landing = destinations(send_dst[group_index]).reshape(-1)
        running = running.at[landing].add(fetched.reshape(-1, feature_width), mode='drop')
        return (running, None)
    gathered, _ = lax.scan(forward_group, jnp.zeros((NODES, feature_width), jnp.float32), group_list)
    aggregated = (features.astype(jnp.float32) + gathered).astype(jnp.bfloat16)
    preact = jnp.dot(aggregated, weight, preferred_element_type=jnp.float32)
    sigmoid = jax.nn.sigmoid(preact)
    output = (preact * sigmoid).astype(jnp.bfloat16)
    pre_grad = (cotangent.astype(jnp.float32) * sigmoid * (1.0 + preact * (1.0 - sigmoid))).astype(jnp.bfloat16)
    grad_w = jnp.dot(aggregated.T, pre_grad, preferred_element_type=jnp.float32) * (1.0 / math.sqrt(NODES))
    back_in = jnp.dot(pre_grad, weight.T, preferred_element_type=jnp.float32).astype(jnp.bfloat16)

    def backward_group(group_index):
        landing = destinations(send_dst[group_index])
        fetched = back_in[jnp.minimum(landing, NODES - 1)]
        keep_source = jnp.where(send_dst[group_index] < ROWS_DEV, send_src[group_index], tile_rows).astype(jnp.int32)
        spread = jax.vmap(place_rows, in_axes=(0, 0, None, None))(keep_source.reshape(REPS, -1), fetched.reshape(REPS, -1, feature_width), tile_rows, feature_width)
        spread = spread.reshape(REPS, CBLK, KPC, BLK, feature_width)
        tile_group = tiles[group_index].astype(jnp.float32)
        return jnp.einsum('cbkij,cbkif->bjf', tile_group, spread).reshape(group_size, feature_width)
    column_terms = lax.map(backward_group, group_list)
    grad_x = (back_in.astype(jnp.float32) + column_terms.reshape(NODES, feature_width)).astype(jnp.bfloat16)
    return (output, grad_w, grad_x)
```

```python
import math

import jax
import jax.numpy as jnp
from jax import lax
from jax.experimental import pallas as pl
from jax.experimental.pallas import tpu as pltpu
from jax.sharding import PartitionSpec as P

BF16 = jnp.bfloat16
F32 = jnp.float32
PAD = 32
LANES = 128


def whole(count):
    return [pl.BlockSpec(memory_space=pltpu.VMEM)] * count


def params(slots):
    return pltpu.CompilerParams(vmem_limit_bytes=(4 << 20) + (16 << 10) * slots)


def dot(a, b, contract_a, contract_b):
    return lax.dot_general(
        a, b, (((contract_a,), (contract_b,)), ((), ())), preferred_element_type=F32
    )


def pick_kernel(source_ref, tiles_ref, picked_ref):
    slots = source_ref.shape[1]
    per_col, block = tiles_ref.shape[1], tiles_ref.shape[2]
    first = pl.program_id(0) * (per_col * block)
    named = jnp.transpose(jnp.broadcast_to(source_ref[...], (LANES, slots))) - first
    lane = lax.broadcasted_iota(jnp.int32, (slots, LANES), 1)
    hot = jnp.concatenate(
        [jnp.where(named == lane + k * LANES, 1.0, 0.0).astype(BF16) for k in range(per_col)],
        axis=1,
    )
    rows = tiles_ref[0].reshape(per_col * block, block)
    picked_ref[0] = dot(hot, rows, 1, 0).astype(BF16)


def partial_kernel(reps, picked_ref, landing_ref, *refs):
    out_ref = refs[-1]
    rep = lax.axis_index("rep")
    total = dot(picked_ref[rep], refs[0][...], 1, 0)
    for step in range(1, reps):
        total += dot(picked_ref[lax.rem(rep + reps - step, reps)], refs[step][...], 1, 0)
    out_ref[...] = total.reshape(out_ref.shape).astype(BF16) + landing_ref[...]


def layer_kernel(
    slot_count, chunk, incoming_ref, features_ref, weight_ref, cotangent_ref, output_ref, back_ref, send_ref
):
    peers, _, width = incoming_ref.shape
    rows = features_ref.shape[0]
    wide = width // PAD
    incoming = incoming_ref[...].reshape(peers * PAD, width)
    groups = pl.cdiv(peers, wide)
    notes = jnp.sum(incoming_ref[:, 16:PAD, :].astype(F32), axis=0)
    row = lax.broadcasted_iota(jnp.int32, (rows, width), 0)
    lane = lax.broadcasted_iota(jnp.int32, (rows, width), 1)
    valid = lax.rem(lane, PAD) < slot_count
    hots = []
    for e in range(groups):
        at = slot_count - 16 + e
        landing = notes[at : at + 1, :].astype(jnp.int32)
        hots.append(jnp.where(valid & (landing == row), 1.0, 0.0).astype(BF16))
    hot = hots[0] if groups == 1 else jnp.concatenate(hots, axis=1)
    hot = hot[:, : peers * PAD]
    weight = weight_ref[...]
    aggregated = (features_ref[...].astype(F32) + dot(hot, incoming, 1, 0)).astype(BF16)
    preact = dot(aggregated, weight, 1, 0)
    sigmoid = jax.nn.sigmoid(preact)
    output_ref[...] = (preact * sigmoid).astype(BF16)
    pre_grad = (
        cotangent_ref[...].astype(F32) * sigmoid * (1.0 + preact * (1.0 - sigmoid))
    ).astype(BF16)
    back_in = dot(pre_grad, weight, 1, 1).astype(BF16)
    back_ref[...] = back_in
    requested = dot(hot, back_in, 0, 0).reshape(peers, PAD, width)
    local_w = dot(aggregated, pre_grad, 0, 0)
    if peers * chunk > width:
        local_w = jnp.concatenate(
            [local_w, jnp.zeros((peers * chunk - width, width), F32)], axis=0
        )
    send_ref[...] = jnp.concatenate(
        [requested, local_w.reshape(peers, chunk, width)], axis=1
    ).astype(BF16)


def terms_kernel(reps, picked_ref, returned_ref, back_ref, kept_ref, *send_refs):
    peers, depth, width = returned_ref.shape
    rep = lax.axis_index("rep")
    rows = returned_ref[:, :PAD, :].reshape(peers * PAD, width)
    part = jnp.sum(returned_ref[:, PAD:, :].astype(F32), axis=0)
    own = dot(picked_ref[rep], rows, 0, 0) + back_ref[...].astype(F32)
    kept_ref[...] = jnp.concatenate([own, part], axis=0)
    for step in range(1, reps):
        term = dot(picked_ref[lax.rem(rep + step, reps)], rows, 0, 0)
        send_refs[step - 1][...] = jnp.concatenate([term, part], axis=0).astype(BF16)


def finish_kernel(reps, peers, kept_ref, *refs):
    got, (grad_x_ref, chunk_ref, parts_ref) = refs[: reps - 1], refs[reps - 1 :]
    rows = grad_x_ref.shape[0]
    rep = lax.axis_index("rep")
    total = kept_ref[:rows, :]
    parts_ref[rep] = kept_ref[rows:, :].astype(BF16).astype(F32)
    for step in range(1, reps):
        arrived = got[step - 1][...].astype(F32)
        total += arrived[:rows]
        parts_ref[lax.rem(rep + reps - step, reps)] = arrived[rows:]
    grad_x_ref[...] = total.astype(BF16)
    chunk = parts_ref[0]
    for other in range(1, reps):
        chunk += parts_ref[other]
    chunk_ref[...] = jnp.broadcast_to(chunk.astype(BF16)[None], chunk_ref.shape)


def local(features, weight, tiles, send_src, send_dst, cotangent):
    blocks = tiles[0, 0]
    source = send_src[0, 0]
    target = send_dst[0, 0]
    peers, slot_count = target.shape
    rows, width = features.shape
    cols, per_col, block = blocks.shape[:3]
    reps = lax.axis_size("rep")
    slots = peers * PAD
    chunk = max(16, width // peers)
    wide = width // PAD
    mine = lax.axis_index("rows")

    def shifted(value, step):
        return lax.ppermute(value, "rep", [(i, (i + step) % reps) for i in range(reps)])

    gathered = [features] + [shifted(features, step) for step in range(1, reps)]

    named = jnp.where(target < rows, source, -1)
    named = jnp.pad(named, ((0, 0), (0, PAD - slot_count)), constant_values=-1).reshape(1, slots)
    picked = pl.pallas_call(
        pick_kernel,
        grid=(cols,),
        out_shape=jax.ShapeDtypeStruct((cols, slots, block), BF16),
        in_specs=[
            pl.BlockSpec((1, slots), lambda b: (0, 0)),
            pl.BlockSpec((1, per_col, block, block), lambda b: (b, 0, 0, 0)),
        ],
        out_specs=pl.BlockSpec((1, slots, block), lambda b: (b, 0, 0)),
        compiler_params=params(slots),
        name="pick",
    )(named, blocks)

    lane = jnp.arange(width)
    tiled = jnp.tile(jnp.pad(target, ((0, 0), (0, PAD - slot_count))), (1, wide))
    tiled = jnp.where(lane // PAD == mine % wide, tiled, 0)
    note_row = jnp.arange(PAD) == slot_count + mine // wide
    landing = jnp.where(note_row[None, :, None], tiled[:, None, :], 0).astype(BF16)

    outgoing = pl.pallas_call(
        lambda *refs: partial_kernel(reps, *refs),
        out_shape=jax.ShapeDtypeStruct((peers, PAD, width), BF16),
        in_specs=whole(2 + reps),
        out_specs=whole(1)[0],
        compiler_params=params(slots),
        name="partial",
    )(picked, landing, *gathered)

    incoming = lax.all_to_all(outgoing, "rows", split_axis=0, concat_axis=0, tiled=True)

    output, back_in, requested = pl.pallas_call(
        lambda *refs: layer_kernel(slot_count, chunk, *refs),
        out_shape=(
            jax.ShapeDtypeStruct((rows, width), BF16),
            jax.ShapeDtypeStruct((rows, width), BF16),
            jax.ShapeDtypeStruct((peers, PAD + chunk, width), BF16),
        ),
        in_specs=whole(4),
        out_specs=tuple(whole(3)),
        compiler_params=params(slots),
        name="layer",
    )(incoming, features, weight, cotangent)

    returned = lax.all_to_all(requested, "rows", split_axis=0, concat_axis=0, tiled=True)

    kept, *sends = pl.pallas_call(
        lambda *refs: terms_kernel(reps, *refs),
        out_shape=(jax.ShapeDtypeStruct((rows + chunk, width), F32),)
        + (jax.ShapeDtypeStruct((rows + chunk, width), BF16),) * (reps - 1),
        in_specs=whole(3),
        out_specs=tuple(whole(reps)),
        compiler_params=params(slots),
        name="terms",
    )(picked, returned, back_in)

    arrived = [shifted(sends[step - 1], step) for step in range(1, reps)]

    grad_x, share = pl.pallas_call(
        lambda *refs: finish_kernel(reps, peers, *refs),
        out_shape=(
            jax.ShapeDtypeStruct((rows, width), BF16),
            jax.ShapeDtypeStruct((peers, chunk, width), BF16),
        ),
        in_specs=whole(reps),
        out_specs=tuple(whole(2)),
        scratch_shapes=[pltpu.VMEM((reps, chunk, width), F32)],
        compiler_params=params(slots),
        name="finish",
    )(kept, *arrived)

    shares = lax.all_to_all(share, "rows", split_axis=0, concat_axis=0, tiled=True)
    node_count = rows * lax.axis_size("rows") * reps
    grad_w = shares.reshape(peers * chunk, width)[:width].astype(F32) * (
        1.0 / math.sqrt(node_count)
    )
    return (output, grad_w, grad_x)


def solution(mesh):
    placed = (
        P(("rows", "rep"), None),
        P(),
        P("rows", "rep", None, None, None, None),
        P("rows", "rep", None, None),
        P("rows", "rep", None, None),
        P(("rows", "rep"), None),
    )
    return jax.shard_map(
        local,
        mesh=mesh,
        in_specs=placed,
        out_specs=(P(("rows", "rep"), None), P(), P(("rows", "rep"), None)),
        check_vma=False,
    )
```

```python
import math

import jax
import jax.numpy as jnp
from jax import lax
from jax.experimental import pallas as pl
from jax.experimental.pallas import tpu as pltpu
from jax.sharding import PartitionSpec as P

BF16 = jnp.bfloat16
F32 = jnp.float32
PAD = 32
LANES = 128
PAIR = 2


def whole(count):
    return [pl.BlockSpec(memory_space=pltpu.VMEM)] * count


def params(slots):
    return pltpu.CompilerParams(vmem_limit_bytes=(4 << 20) + (16 << 10) * slots)


def dot(a, b, contract_a, contract_b):
    return lax.dot_general(
        a, b, (((contract_a,), (contract_b,)), ((), ())), preferred_element_type=F32
    )


def target_of(index, step, count):
    if count & (count - 1) == 0:
        return index ^ step
    return lax.rem(index + step, count) if isinstance(index, jax.Array) else (index + step) % count


def origin_of(index, step, count):
    if count & (count - 1) == 0:
        return index ^ step
    return lax.rem(index + count - step, count)


def step_to(index, other, count):
    if count & (count - 1) == 0:
        return index ^ other
    return lax.rem(other + count - index, count)


def place(step, mate, chips, wide):
    at = mate * chips + step
    return at // wide, at % wide


def pick_kernel(source_ref, tiles_ref, picked_ref):
    slots = source_ref.shape[1]
    per_col, block = tiles_ref.shape[1], tiles_ref.shape[2]
    first = pl.program_id(0) * (per_col * block)
    named = jnp.transpose(jnp.broadcast_to(source_ref[...], (LANES, slots))) - first
    lane = lax.broadcasted_iota(jnp.int32, (slots, LANES), 1)
    hot = jnp.concatenate(
        [jnp.where(named == lane + k * LANES, 1.0, 0.0).astype(BF16) for k in range(per_col)],
        axis=1,
    )
    rows = tiles_ref[0].reshape(per_col * block, block)
    picked_ref[0] = dot(hot, rows, 1, 0).astype(BF16)


def partial_kernel(reps, chips, picked_ref, landing_ref, *refs):
    features, sends, total_ref = refs[:reps], refs[reps:-1], refs[-1]
    rep = lax.axis_index("rep")
    chip = lax.div(lax.axis_index("rows"), PAIR)
    depth = PAIR * PAD
    total = landing_ref[...].astype(F32)
    for step in range(reps):
        total += dot(picked_ref[origin_of(rep, step, reps)], features[step][...], 1, 0)
    total_ref[...] = total
    for step in range(chips):
        first = pl.multiple_of(target_of(chip, step, chips) * depth, depth)
        sends[step][...] = total_ref[pl.ds(first, depth), :].astype(BF16)


def layer_kernel(chips, slot_count, chunk, *refs):
    got, refs = refs[: PAIR * chips], refs[PAIR * chips :]
    features_ref, mate_features_ref, cotangent_ref, mate_cotangent_ref, weight_ref = refs[:5]
    output_ref, back_ref, *sends, grad_ref = refs[5:]
    rows, width = features_ref.shape
    wide = width // PAD
    core = lax.rem(lax.axis_index("rows"), PAIR)
    chip = lax.div(lax.axis_index("rows"), PAIR)
    groups = pl.cdiv(PAIR * chips, wide)
    row = lax.broadcasted_iota(jnp.int32, (rows, width), 0)
    lane = lax.broadcasted_iota(jnp.int32, (rows, width), 1)
    valid = lax.rem(lane, PAD) < slot_count
    weight = weight_ref[...]
    hots, aggregates = [], []
    for half, own in ((core, features_ref), (1 - core, mate_features_ref)):
        first = pl.multiple_of(half * PAD, PAD)
        blocks = [ref[pl.ds(first, PAD), :] for ref in got]
        notes = [jnp.zeros((1, width), F32)] * groups
        for at, block in enumerate(blocks):
            mate = at // chips
            notes[at // wide] += block[16:].astype(F32)[slot_count - 16 + mate :][:1]
        parts = [
            jnp.where(valid & (note.astype(jnp.int32) == row), 1.0, 0.0).astype(BF16)
            for note in notes
        ]
        hot = parts[0] if groups == 1 else jnp.concatenate(parts, axis=1)
        hot = hot[:, : PAIR * chips * PAD]
        arrived = dot(hot, jnp.concatenate(blocks, axis=0), 1, 0)
        hots.append(hot[:, : chips * PAD])
        aggregates.append((own[...].astype(F32) + arrived).astype(BF16))
    aggregated = jnp.concatenate(aggregates, axis=0)
    preact = dot(aggregated, weight, 1, 0)
    sigmoid = jax.nn.sigmoid(preact)
    output_ref[...] = (preact * sigmoid)[:rows].astype(BF16)
    cotangent = jnp.concatenate([cotangent_ref[...], mate_cotangent_ref[...]], axis=0)
    pre_grad = (cotangent.astype(F32) * sigmoid * (1.0 + preact * (1.0 - sigmoid))).astype(BF16)
    back_in = dot(pre_grad, weight, 1, 1).astype(BF16)
    back_ref[...] = back_in[:rows]
    grad_ref[:width] = dot(aggregated, pre_grad, 0, 0)
    if grad_ref.shape[0] > width:
        grad_ref[width:] = jnp.zeros((grad_ref.shape[0] - width, width), F32)
    asked = [dot(hot, back_in[h * rows : (h + 1) * rows], 0, 0) for h, hot in enumerate(hots)]
    for step in range(chips):
        from_own, from_mate = (part[step * PAD : (step + 1) * PAD].astype(BF16) for part in asked)
        first = target_of(chip, step, chips) * PAIR + core
        first = pl.multiple_of(first * chunk, chunk)
        sends[step][pl.ds(pl.multiple_of(core * PAD, PAD), PAD), :] = from_own
        sends[step][pl.ds(pl.multiple_of((1 - core) * PAD, PAD), PAD), :] = from_mate
        sends[step][PAIR * PAD :, :] = grad_ref[pl.ds(first, chunk), :].astype(BF16)


def terms_kernel(reps, chips, picked_ref, back_ref, *refs):
    returned, kept_ref, sends, rows_ref = refs[:chips], refs[chips], refs[chips + 1 : -1], refs[-1]
    rep = lax.axis_index("rep")
    chip = lax.div(lax.axis_index("rows"), PAIR)
    depth = PAIR * PAD
    part = returned[0][depth:, :].astype(F32)
    for step in range(1, chips):
        part += returned[step][depth:, :].astype(F32)
    for step in range(chips):
        first = pl.multiple_of(origin_of(chip, step, chips) * depth, depth)
        rows_ref[pl.ds(first, depth), :] = returned[step][:depth, :]
    rows = rows_ref[...]
    own = dot(picked_ref[rep], rows, 0, 0) + back_ref[...].astype(F32)
    kept_ref[...] = jnp.concatenate([own, part], axis=0)
    for step in range(1, reps):
        term = dot(picked_ref[lax.rem(rep + step, reps)], rows, 0, 0)
        sends[step - 1][...] = jnp.concatenate([term, part], axis=0).astype(BF16)


def finish_kernel(reps, kept_ref, *refs):
    got, (grad_x_ref, chunk_ref, parts_ref) = refs[: reps - 1], refs[reps - 1 :]
    rows = grad_x_ref.shape[0]
    rep = lax.axis_index("rep")
    total = kept_ref[:rows, :]
    parts_ref[rep] = kept_ref[rows:, :].astype(BF16).astype(F32)
    for step in range(1, reps):
        arrived = got[step - 1][...].astype(F32)
        total += arrived[:rows]
        parts_ref[lax.rem(rep + reps - step, reps)] = arrived[rows:]
    grad_x_ref[...] = total.astype(BF16)
    chunk = parts_ref[0]
    for other in range(1, reps):
        chunk += parts_ref[other]
    chunk_ref[...] = jnp.broadcast_to(chunk.astype(BF16)[None], chunk_ref.shape)


def local(features, weight, tiles, send_src, send_dst, cotangent):
    blocks = tiles[0, 0]
    source = send_src[0, 0]
    target = send_dst[0, 0]
    peers, slot_count = target.shape
    rows, width = features.shape
    cols, per_col, block = blocks.shape[:3]
    reps = lax.axis_size("rep")
    chips = peers // PAIR
    slots = peers * PAD
    chunk = max(16, width // peers)
    wide = width // PAD
    chip = lax.axis_index("rows") // PAIR

    def over_rep(value, step):
        return lax.ppermute(value, "rep", [(i, target_of(i, step, reps)) for i in range(reps)])

    def over_chips(value, step):
        pairs = [
            (i * PAIR + core, target_of(i, step, chips) * PAIR + core)
            for i in range(chips)
            for core in range(PAIR)
        ]
        return lax.ppermute(value, "rows", pairs)

    def to_mate(value):
        return lax.ppermute(value, "rows", [(i, i ^ 1) for i in range(peers)])

    gathered = [features] + [over_rep(features, step) for step in range(1, reps)]

    named = jnp.where(target < rows, source, -1)
    named = jnp.pad(named, ((0, 0), (0, PAD - slot_count)), constant_values=-1).reshape(1, slots)
    picked = pl.pallas_call(
        pick_kernel,
        grid=(cols,),
        out_shape=jax.ShapeDtypeStruct((cols, slots, block), BF16),
        in_specs=[
            pl.BlockSpec((1, slots), lambda b: (0, 0)),
            pl.BlockSpec((1, per_col, block, block), lambda b: (b, 0, 0, 0)),
        ],
        out_specs=pl.BlockSpec((1, slots, block), lambda b: (b, 0, 0)),
        compiler_params=params(slots),
        name="pick",
    )(named, blocks)

    tiled = jnp.tile(jnp.pad(target, ((0, 0), (0, PAD - slot_count))), (1, wide))
    at = step_to(chip, jnp.arange(peers) // PAIR, chips)
    row, lane = jnp.arange(PAD)[None, :, None], jnp.arange(width)[None, None, :]
    noted = jnp.zeros((), jnp.bool_)
    for mate in range(PAIR):
        spot = (mate * chips + at[:, None, None]) % wide
        noted = noted | ((row == slot_count + mate) & (lane // PAD == spot))
    landing = jnp.where(noted, tiled[:, None, :], 0).astype(BF16).reshape(slots, width)

    message = jax.ShapeDtypeStruct((PAIR * PAD, width), BF16)
    outgoing = pl.pallas_call(
        lambda *refs: partial_kernel(reps, chips, *refs),
        out_shape=(message,) * chips,
        in_specs=whole(2 + reps),
        out_specs=tuple(whole(chips)),
        scratch_shapes=[pltpu.VMEM((slots, width), F32)],
        compiler_params=params(slots),
        name="partial",
    )(picked, landing, *gathered)

    direct = [outgoing[0]] + [over_chips(outgoing[step], step) for step in range(1, chips)]
    shared = [to_mate(value) for value in direct]
    early_features, early_cotangent, _ = lax.optimization_barrier(
        (features, cotangent, outgoing[0])
    )

    output, back_in, *requested = pl.pallas_call(
        lambda *refs: layer_kernel(chips, slot_count, chunk, *refs),
        out_shape=(
            jax.ShapeDtypeStruct((rows, width), BF16),
            jax.ShapeDtypeStruct((rows, width), BF16),
        )
        + (jax.ShapeDtypeStruct((PAIR * PAD + chunk, width), BF16),) * chips,
        in_specs=whole(PAIR * chips + 5),
        out_specs=tuple(whole(2 + chips)),
        scratch_shapes=[pltpu.VMEM((max(width, peers * chunk), width), F32)],
        compiler_params=params(slots),
        name="layer",
    )(
        *direct,
        *shared,
        features,
        to_mate(early_features),
        cotangent,
        to_mate(early_cotangent),
        weight,
    )

    returned = [requested[0]] + [over_chips(requested[step], step) for step in range(1, chips)]

    kept, *sends = pl.pallas_call(
        lambda *refs: terms_kernel(reps, chips, *refs),
        out_shape=(jax.ShapeDtypeStruct((rows + chunk, width), F32),)
        + (jax.ShapeDtypeStruct((rows + chunk, width), BF16),) * (reps - 1),
        in_specs=whole(2 + chips),
        out_specs=tuple(whole(reps)),
        scratch_shapes=[pltpu.VMEM((slots, width), BF16)],
        compiler_params=params(slots),
        name="terms",
    )(picked, back_in, *returned)

    arrived = [
        lax.ppermute(sends[step - 1], "rep", [(i, (i + step) % reps) for i in range(reps)])
        for step in range(1, reps)
    ]

    grad_x, share = pl.pallas_call(
        lambda *refs: finish_kernel(reps, *refs),
        out_shape=(
            jax.ShapeDtypeStruct((rows, width), BF16),
            jax.ShapeDtypeStruct((peers, chunk, width), BF16),
        ),
        in_specs=whole(reps),
        out_specs=tuple(whole(2)),
        scratch_shapes=[pltpu.VMEM((reps, chunk, width), F32)],
        compiler_params=params(slots),
        name="finish",
    )(kept, *arrived)

    shares = lax.all_to_all(share, "rows", split_axis=0, concat_axis=0, tiled=True)
    node_count = rows * lax.axis_size("rows") * reps
    grad_w = shares.reshape(peers * chunk, width)[:width].astype(F32) * (
        1.0 / math.sqrt(node_count)
    )
    return (output, grad_w, grad_x)


def solution(mesh):
    placed = (
        P(("rows", "rep"), None),
        P(),
        P("rows", "rep", None, None, None, None),
        P("rows", "rep", None, None),
        P("rows", "rep", None, None),
        P(("rows", "rep"), None),
    )
    return jax.shard_map(
        local,
        mesh=mesh,
        in_specs=placed,
        out_specs=(P(("rows", "rep"), None), P(), P(("rows", "rep"), None)),
        check_vma=False,
    )
```

```python
import math

import jax
import jax.numpy as jnp
from jax import lax
from jax.experimental import pallas as pl
from jax.experimental.pallas import tpu as pltpu
from jax.sharding import PartitionSpec as P

BF16 = jnp.bfloat16
F32 = jnp.float32
PAD = 32
LANES = 128
PAIR = 2


def whole(count):
    return [pl.BlockSpec(memory_space=pltpu.VMEM)] * count


def params(slots):
    return pltpu.CompilerParams(vmem_limit_bytes=(4 << 20) + (16 << 10) * slots)


def dot(a, b, contract_a, contract_b):
    return lax.dot_general(
        a, b, (((contract_a,), (contract_b,)), ((), ())), preferred_element_type=F32
    )


def target_of(index, step, count):
    if count & (count - 1) == 0:
        return index ^ step
    return lax.rem(index + step, count) if isinstance(index, jax.Array) else (index + step) % count


def origin_of(index, step, count):
    if count & (count - 1) == 0:
        return index ^ step
    return lax.rem(index + count - step, count)


def step_to(index, other, count):
    if count & (count - 1) == 0:
        return index ^ other
    return lax.rem(other + count - index, count)


def place(step, mate, chips, wide):
    at = mate * chips + step
    return at // wide, at % wide


def pick_kernel(source_ref, tiles_ref, picked_ref):
    slots = source_ref.shape[1]
    per_col, block = tiles_ref.shape[1], tiles_ref.shape[2]
    first = pl.program_id(0) * (per_col * block)
    named = jnp.transpose(jnp.broadcast_to(source_ref[...], (LANES, slots))) - first
    lane = lax.broadcasted_iota(jnp.int32, (slots, LANES), 1)
    hot = jnp.concatenate(
        [jnp.where(named == lane + k * LANES, 1.0, 0.0).astype(BF16) for k in range(per_col)],
        axis=1,
    )
    rows = tiles_ref[0].reshape(per_col * block, block)
    picked_ref[0] = dot(hot, rows, 1, 0).astype(BF16)


def partial_kernel(reps, chips, picked_ref, landing_ref, *refs):
    features, sends, total_ref = refs[:reps], refs[reps:-1], refs[-1]
    rep = lax.axis_index("rep")
    chip = lax.div(lax.axis_index("rows"), PAIR)
    depth = PAIR * PAD
    total = landing_ref[...].astype(F32)
    for step in range(reps):
        total += dot(picked_ref[origin_of(rep, step, reps)], features[step][...], 1, 0)
    total_ref[...] = total
    for step in range(chips):
        first = pl.multiple_of(target_of(chip, step, chips) * depth, depth)
        sends[step][...] = total_ref[pl.ds(first, depth), :].astype(BF16)


def layer_kernel(chips, slot_count, chunk, *refs):
    got, refs = refs[: PAIR * chips], refs[PAIR * chips :]
    features_ref, mate_features_ref, cotangent_ref, mate_cotangent_ref, weight_ref = refs[:5]
    output_ref, back_ref, *sends, grad_ref = refs[5:]
    rows, width = features_ref.shape
    wide = width // PAD
    core = lax.rem(lax.axis_index("rows"), PAIR)
    chip = lax.div(lax.axis_index("rows"), PAIR)
    groups = pl.cdiv(PAIR * chips, wide)
    row = lax.broadcasted_iota(jnp.int32, (rows, width), 0)
    lane = lax.broadcasted_iota(jnp.int32, (rows, width), 1)
    valid = lax.rem(lane, PAD) < slot_count
    weight = weight_ref[...]
    hots, aggregates = [], []
    for half, own in ((core, features_ref), (1 - core, mate_features_ref)):
        first = pl.multiple_of(half * PAD, PAD)
        blocks = [ref[pl.ds(first, PAD), :] for ref in got]
        notes = [jnp.zeros((1, width), F32)] * groups
        for at, block in enumerate(blocks):
            mate = at // chips
            notes[at // wide] += block[16:].astype(F32)[slot_count - 16 + mate :][:1]
        parts = [
            jnp.where(valid & (note.astype(jnp.int32) == row), 1.0, 0.0).astype(BF16)
            for note in notes
        ]
        hot = parts[0] if groups == 1 else jnp.concatenate(parts, axis=1)
        hot = hot[:, : PAIR * chips * PAD]
        arrived = dot(hot, jnp.concatenate(blocks, axis=0), 1, 0)
        hots.append(hot[:, : chips * PAD])
        aggregates.append((own[...].astype(F32) + arrived).astype(BF16))
    aggregated = jnp.concatenate(aggregates, axis=0)
    preact = dot(aggregated, weight, 1, 0)
    sigmoid = jax.nn.sigmoid(preact)
    output_ref[...] = (preact * sigmoid)[:rows].astype(BF16)
    cotangent = jnp.concatenate([cotangent_ref[...], mate_cotangent_ref[...]], axis=0)
    pre_grad = (cotangent.astype(F32) * sigmoid * (1.0 + preact * (1.0 - sigmoid))).astype(BF16)
    back_in = dot(pre_grad, weight, 1, 1).astype(BF16)
    back_ref[...] = back_in[:rows]
    grad_ref[:width] = dot(aggregated, pre_grad, 0, 0)
    if grad_ref.shape[0] > width:
        grad_ref[width:] = jnp.zeros((grad_ref.shape[0] - width, width), F32)
    asked = [dot(hot, back_in[h * rows : (h + 1) * rows], 0, 0) for h, hot in enumerate(hots)]
    for step in range(chips):
        from_own, from_mate = (part[step * PAD : (step + 1) * PAD].astype(BF16) for part in asked)
        first = target_of(chip, step, chips) * PAIR + core
        first = pl.multiple_of(first * chunk, chunk)
        sends[step][pl.ds(pl.multiple_of(core * PAD, PAD), PAD), :] = from_own
        sends[step][pl.ds(pl.multiple_of((1 - core) * PAD, PAD), PAD), :] = from_mate
        sends[step][PAIR * PAD :, :] = grad_ref[pl.ds(first, chunk), :].astype(BF16)


def terms_kernel(reps, chips, picked_ref, back_ref, *refs):
    returned, kept_ref, sends, rows_ref = refs[:chips], refs[chips], refs[chips + 1 : -1], refs[-1]
    rep = lax.axis_index("rep")
    chip = lax.div(lax.axis_index("rows"), PAIR)
    depth = PAIR * PAD
    part = returned[0][depth:, :].astype(F32)
    for step in range(1, chips):
        part += returned[step][depth:, :].astype(F32)
    for step in range(chips):
        first = pl.multiple_of(origin_of(chip, step, chips) * depth, depth)
        rows_ref[pl.ds(first, depth), :] = returned[step][:depth, :]
    rows = rows_ref[...]
    own = dot(picked_ref[rep], rows, 0, 0) + back_ref[...].astype(F32)
    kept_ref[...] = jnp.concatenate([own, part], axis=0)
    for step in range(1, reps):
        term = dot(picked_ref[lax.rem(rep + step, reps)], rows, 0, 0)
        sends[step - 1][...] = jnp.concatenate([term, part], axis=0).astype(BF16)


def chunk_kernel(reps, kept_ref, *refs):
    got, (chunk_ref, parts_ref) = refs[: reps - 1], refs[reps - 1 :]
    depth = chunk_ref.shape[0]
    rows = kept_ref.shape[0] - depth
    rep = lax.axis_index("rep")
    parts_ref[rep] = kept_ref[rows:, :].astype(BF16).astype(F32)
    for step in range(1, reps):
        parts_ref[lax.rem(rep + reps - step, reps)] = got[step - 1][rows:, :].astype(F32)
    chunk = parts_ref[0]
    for other in range(1, reps):
        chunk += parts_ref[other]
    chunk_ref[...] = chunk.astype(BF16)


def grad_x_kernel(kept_ref, *refs):
    got, grad_x_ref = refs[:-1], refs[-1]
    rows = grad_x_ref.shape[0]
    total = kept_ref[:rows, :]
    for ref in got:
        total += ref[:rows, :].astype(F32)
    grad_x_ref[...] = total.astype(BF16)


def grad_w_kernel(chips, scale, *refs):
    got, grad_w_ref = refs[:-1], refs[-1]
    chunk = got[0].shape[0]
    core = lax.rem(lax.axis_index("rows"), PAIR)
    chip = lax.div(lax.axis_index("rows"), PAIR)
    for at, ref in enumerate(got):
        half = core if at < chips else 1 - core
        first = (origin_of(chip, at % chips, chips) * PAIR + half) * chunk
        grad_w_ref[pl.ds(pl.multiple_of(first, chunk), chunk), :] = ref[...].astype(F32) * scale


def local(features, weight, tiles, send_src, send_dst, cotangent):
    blocks = tiles[0, 0]
    source = send_src[0, 0]
    target = send_dst[0, 0]
    peers, slot_count = target.shape
    rows, width = features.shape
    cols, per_col, block = blocks.shape[:3]
    reps = lax.axis_size("rep")
    chips = peers // PAIR
    slots = peers * PAD
    chunk = max(16, width // peers)
    wide = width // PAD
    chip = lax.axis_index("rows") // PAIR

    def over_rep(value, step):
        return lax.ppermute(value, "rep", [(i, target_of(i, step, reps)) for i in range(reps)])

    def over_chips(value, step):
        pairs = [
            (i * PAIR + core, target_of(i, step, chips) * PAIR + core)
            for i in range(chips)
            for core in range(PAIR)
        ]
        return lax.ppermute(value, "rows", pairs)

    def to_mate(value):
        return lax.ppermute(value, "rows", [(i, i ^ 1) for i in range(peers)])

    gathered = [features] + [over_rep(features, step) for step in range(1, reps)]

    named = jnp.where(target < rows, source, -1)
    named = jnp.pad(named, ((0, 0), (0, PAD - slot_count)), constant_values=-1).reshape(1, slots)
    picked = pl.pallas_call(
        pick_kernel,
        grid=(cols,),
        out_shape=jax.ShapeDtypeStruct((cols, slots, block), BF16),
        in_specs=[
            pl.BlockSpec((1, slots), lambda b: (0, 0)),
            pl.BlockSpec((1, per_col, block, block), lambda b: (b, 0, 0, 0)),
        ],
        out_specs=pl.BlockSpec((1, slots, block), lambda b: (b, 0, 0)),
        compiler_params=params(slots),
        name="pick",
    )(named, blocks)

    tiled = jnp.tile(jnp.pad(target, ((0, 0), (0, PAD - slot_count))), (1, wide))
    at = step_to(chip, jnp.arange(peers) // PAIR, chips)
    row, lane = jnp.arange(PAD)[None, :, None], jnp.arange(width)[None, None, :]
    noted = jnp.zeros((), jnp.bool_)
    for mate in range(PAIR):
        spot = (mate * chips + at[:, None, None]) % wide
        noted = noted | ((row == slot_count + mate) & (lane // PAD == spot))
    landing = jnp.where(noted, tiled[:, None, :], 0).astype(BF16).reshape(slots, width)

    message = jax.ShapeDtypeStruct((PAIR * PAD, width), BF16)
    outgoing = pl.pallas_call(
        lambda *refs: partial_kernel(reps, chips, *refs),
        out_shape=(message,) * chips,
        in_specs=whole(2 + reps),
        out_specs=tuple(whole(chips)),
        scratch_shapes=[pltpu.VMEM((slots, width), F32)],
        compiler_params=params(slots),
        name="partial",
    )(picked, landing, *gathered)

    direct = [outgoing[0]] + [over_chips(outgoing[step], step) for step in range(1, chips)]
    shared = [to_mate(value) for value in direct]
    early_features, early_cotangent, _ = lax.optimization_barrier(
        (features, cotangent, outgoing[0])
    )

    output, back_in, *requested = pl.pallas_call(
        lambda *refs: layer_kernel(chips, slot_count, chunk, *refs),
        out_shape=(
            jax.ShapeDtypeStruct((rows, width), BF16),
            jax.ShapeDtypeStruct((rows, width), BF16),
        )
        + (jax.ShapeDtypeStruct((PAIR * PAD + chunk, width), BF16),) * chips,
        in_specs=whole(PAIR * chips + 5),
        out_specs=tuple(whole(2 + chips)),
        scratch_shapes=[pltpu.VMEM((max(width, peers * chunk), width), F32)],
        compiler_params=params(slots),
        name="layer",
    )(
        *direct,
        *shared,
        features,
        to_mate(early_features),
        cotangent,
        to_mate(early_cotangent),
        weight,
    )

    returned = [requested[0]] + [over_chips(requested[step], step) for step in range(1, chips)]

    kept, *sends = pl.pallas_call(
        lambda *refs: terms_kernel(reps, chips, *refs),
        out_shape=(jax.ShapeDtypeStruct((rows + chunk, width), F32),)
        + (jax.ShapeDtypeStruct((rows + chunk, width), BF16),) * (reps - 1),
        in_specs=whole(2 + chips),
        out_specs=tuple(whole(reps)),
        scratch_shapes=[pltpu.VMEM((slots, width), BF16)],
        compiler_params=params(slots),
        name="terms",
    )(picked, back_in, *returned)

    arrived = [
        lax.ppermute(sends[step - 1], "rep", [(i, (i + step) % reps) for i in range(reps)])
        for step in range(1, reps)
    ]

    share = pl.pallas_call(
        lambda *refs: chunk_kernel(reps, *refs),
        out_shape=jax.ShapeDtypeStruct((chunk, width), BF16),
        in_specs=whole(reps),
        out_specs=whole(1)[0],
        scratch_shapes=[pltpu.VMEM((reps, chunk, width), F32)],
        compiler_params=params(slots),
        name="chunk",
    )(kept, *arrived)

    shares = [share] + [over_chips(share, step) for step in range(1, chips)]
    shares += [to_mate(value) for value in shares]

    grad_x = pl.pallas_call(
        grad_x_kernel,
        out_shape=jax.ShapeDtypeStruct((rows, width), BF16),
        in_specs=whole(reps),
        out_specs=whole(1)[0],
        compiler_params=params(slots),
        name="grad_x",
    )(kept, *arrived)

    node_count = rows * lax.axis_size("rows") * reps
    grad_w = pl.pallas_call(
        lambda *refs: grad_w_kernel(chips, 1.0 / math.sqrt(node_count), *refs),
        out_shape=jax.ShapeDtypeStruct((peers * chunk, width), F32),
        in_specs=whole(PAIR * chips),
        out_specs=whole(1)[0],
        compiler_params=params(slots),
        name="grad_w",
    )(*shares)[:width]
    return (output, grad_w, grad_x)


def solution(mesh):
    placed = (
        P(("rows", "rep"), None),
        P(),
        P("rows", "rep", None, None, None, None),
        P("rows", "rep", None, None),
        P("rows", "rep", None, None),
        P(("rows", "rep"), None),
    )
    return jax.shard_map(
        local,
        mesh=mesh,
        in_specs=placed,
        out_specs=(P(("rows", "rep"), None), P(), P(("rows", "rep"), None)),
        check_vma=False,
    )
```

```python
import math

import jax
import jax.numpy as jnp
from jax import lax
from jax.experimental import pallas as pl
from jax.experimental.pallas import tpu as pltpu
from jax.sharding import PartitionSpec as P

BF16 = jnp.bfloat16
F32 = jnp.float32
PAD = 32
LANES = 128
PAIR = 2


def whole(count):
    return [pl.BlockSpec(memory_space=pltpu.VMEM)] * count


def params(slots):
    return pltpu.CompilerParams(vmem_limit_bytes=(4 << 20) + (16 << 10) * slots)


def dot(a, b, contract_a, contract_b):
    return lax.dot_general(
        a, b, (((contract_a,), (contract_b,)), ((), ())), preferred_element_type=F32
    )


LOW, HIGH, BOTH = (1, 0, 3, 2), (2, 3, 0, 1), (3, 2, 1, 0)
PLAN = dict(
    A=(LOW, BOTH, HIGH), B=(BOTH, LOW, HIGH), C=(LOW, HIGH, BOTH), D=(HIGH, LOW, BOTH)
)


def targets(name, step, count):
    if step == 0:
        return tuple(range(count))
    if count == len(PLAN[name]) + 1:
        return PLAN[name][step - 1]
    return tuple((i + step) % count for i in range(count))


def entry(table, index):
    found = table[0]
    for i in range(1, len(table)):
        found = jnp.where(index == i, table[i], found)
    return found


def target_of(name, index, step, count):
    return entry(targets(name, step, count), index)


def origin_of(name, index, step, count):
    sent = targets(name, step, count)
    return entry(tuple(sent.index(i) for i in range(count)), index)


def step_to(name, index, other, count):
    found = jnp.zeros_like(other)
    for step in range(1, count):
        found = jnp.where(target_of(name, index, step, count) == other, step, found)
    return found


def asked_at(step, count):
    back = targets("C", step, count)
    for at in range(count):
        there = targets("B", at, count)
        if all(there[back[i]] == i for i in range(count)):
            return at
    raise ValueError("B and C differ")


def inputs_kernel(
    chips, source_ref, target_ref, features_ref, tiles_ref, picked_ref, base_ref, held, named_ref, sems
):
    cols, per_col, block = held.shape[:3]
    copies = [pltpu.make_async_copy(tiles_ref.at[b], held.at[b], sems.at[b]) for b in range(cols)]
    for copy in copies:
        copy.start()
    peers, slot_count = source_ref.shape
    slots, width = base_ref.shape
    wide = width // PAD
    chip = lax.div(lax.axis_index("rows"), PAIR)
    target = target_ref[...]
    named_ref[...] = jnp.full(named_ref.shape, -1, jnp.int32)
    named_ref[:, :slot_count] = jnp.where(target < features_ref.shape[0], source_ref[...], -1)
    spread = jnp.broadcast_to(named_ref[...][:, None, :], (peers, PAD, LANES)).reshape(slots, LANES)
    slot = lax.rem(lax.broadcasted_iota(jnp.int32, (slots, LANES), 0), PAD)
    lane = lax.broadcasted_iota(jnp.int32, (slots, LANES), 1)
    column = jnp.sum(jnp.where(lane == slot, spread, 0).astype(F32), axis=1, keepdims=True)
    offset = jnp.broadcast_to(column, (slots, LANES)) - lane.astype(F32)

    named_ref[...] = jnp.zeros(named_ref.shape, jnp.int32)
    named_ref[:, :slot_count] = target
    notes = named_ref[...]
    tiled = notes
    for turn in range(1, LANES // PAD):
        tiled += pltpu.roll(notes, turn * PAD, 1)
    tiled = jnp.concatenate([tiled] * (width // LANES), axis=1)
    tiled = jnp.broadcast_to(tiled[:, None, :], (peers, PAD, width)).reshape(slots, width)
    row = lax.broadcasted_iota(jnp.int32, (slots, width), 0)
    spot = lax.div(lax.broadcasted_iota(jnp.int32, (slots, width), 1), PAD)
    at = step_to("B", chip, lax.div(row, PAD * PAIR), chips)
    keep = jnp.zeros((slots, width), jnp.bool_)
    for mate in range(PAIR):
        here = lax.rem(row, PAD) == slot_count + mate
        keep = keep | (here & (lax.rem(mate * chips + at, wide) == spot))
    landing = jnp.where(keep, tiled, 0).astype(F32)

    for b in range(cols):
        first = b * per_col
        hot = jnp.concatenate(
            [
                jnp.where(offset == float((first + k) * block), 1.0, 0.0).astype(BF16)
                for k in range(per_col)
            ],
            axis=1,
        )
        copies[b].wait()
        rows = held[b].reshape(per_col * block, block)
        picked_ref[b] = dot(hot, rows, 1, 0).astype(BF16)
    base_ref[...] = landing + dot(picked_ref[lax.axis_index("rep")], features_ref[...], 1, 0)


def partial_kernel(reps, chips, picked_ref, base_ref, *refs):
    features, sends, total_ref = refs[: reps - 1], refs[reps - 1 : -1], refs[-1]
    rep = lax.axis_index("rep")
    chip = lax.div(lax.axis_index("rows"), PAIR)
    depth = PAIR * PAD
    total = base_ref[...]
    for step in range(1, reps):
        total += dot(picked_ref[origin_of("A", rep, step, reps)], features[step - 1][...], 1, 0)
    total_ref[...] = total
    for step in range(chips):
        first = pl.multiple_of(target_of("B", chip, step, chips) * depth, depth)
        sends[step][...] = total_ref[pl.ds(first, depth), :].astype(BF16)


def layer_kernel(chips, slot_count, *refs):
    got, refs = refs[: PAIR * chips], refs[PAIR * chips :]
    features_ref, mate_features_ref, cotangent_ref, mate_cotangent_ref, weight_ref = refs[:5]
    output_ref, back_ref, *sends, grad_ref = refs[5:]
    rows, width = features_ref.shape
    wide = width // PAD
    core = lax.rem(lax.axis_index("rows"), PAIR)
    groups = pl.cdiv(PAIR * chips, wide)
    row = lax.broadcasted_iota(jnp.int32, (rows, width), 0)
    lane = lax.broadcasted_iota(jnp.int32, (rows, width), 1)
    valid = lax.rem(lane, PAD) < slot_count
    weight = weight_ref[...]
    hots, aggregates = [], []
    for half, own in ((core, features_ref), (1 - core, mate_features_ref)):
        first = pl.multiple_of(half * PAD, PAD)
        blocks = [ref[pl.ds(first, PAD), :] for ref in got]
        notes = [jnp.zeros((1, width), F32)] * groups
        for at, block in enumerate(blocks):
            mate = at // chips
            notes[at // wide] += block[16:].astype(F32)[slot_count - 16 + mate :][:1]
        parts = [
            jnp.where(valid & (note.astype(jnp.int32) == row), 1.0, 0.0).astype(BF16)
            for note in notes
        ]
        hot = parts[0] if groups == 1 else jnp.concatenate(parts, axis=1)
        hot = hot[:, : PAIR * chips * PAD]
        arrived = dot(hot, jnp.concatenate(blocks, axis=0), 1, 0)
        hots.append(hot[:, : chips * PAD])
        aggregates.append((own[...].astype(F32) + arrived).astype(BF16))
    aggregated = jnp.concatenate(aggregates, axis=0)
    preact = dot(aggregated, weight, 1, 0)
    sigmoid = jax.nn.sigmoid(preact)
    output_ref[...] = (preact * sigmoid)[:rows].astype(BF16)
    cotangent = jnp.concatenate([cotangent_ref[...], mate_cotangent_ref[...]], axis=0)
    pre_grad = (cotangent.astype(F32) * sigmoid * (1.0 + preact * (1.0 - sigmoid))).astype(BF16)
    back_in = dot(pre_grad, weight, 1, 1).astype(BF16)
    back_ref[...] = back_in[:rows]
    grad_ref[...] = dot(aggregated, pre_grad, 0, 0)
    part = width // PAIR
    grad = grad_ref[pl.ds(pl.multiple_of(core * part, part), part), :].astype(BF16)
    asked = [dot(hot, back_in[h * rows : (h + 1) * rows], 0, 0) for h, hot in enumerate(hots)]
    for step in range(chips):
        first = asked_at(step, chips) * PAD
        from_own, from_mate = (part[first : first + PAD].astype(BF16) for part in asked)
        sends[step][pl.ds(pl.multiple_of(core * PAD, PAD), PAD), :] = from_own
        sends[step][pl.ds(pl.multiple_of((1 - core) * PAD, PAD), PAD), :] = from_mate
        sends[step][PAIR * PAD :, :] = grad


def terms_kernel(reps, chips, picked_ref, back_ref, *refs):
    returned, kept_ref, sends = refs[:chips], refs[chips], refs[chips + 1 : -2]
    rows_ref, parts_ref = refs[-2:]
    rep = lax.axis_index("rep")
    chip = lax.div(lax.axis_index("rows"), PAIR)
    depth = PAIR * PAD
    for step in range(chips):
        origin = origin_of("C", chip, step, chips)
        rows_ref[pl.ds(pl.multiple_of(origin * depth, depth), depth), :] = returned[step][:depth, :]
        parts_ref[origin] = returned[step][depth:, :].astype(F32)
    part = parts_ref[0]
    for other in range(1, chips):
        part += parts_ref[other]
    rows = rows_ref[...]
    for step in range(1, reps):
        term = dot(picked_ref[target_of("D", rep, step, reps)], rows, 0, 0)
        sends[step - 1][...] = jnp.concatenate([term, part], axis=0).astype(BF16)
    own = dot(picked_ref[rep], rows, 0, 0) + back_ref[...].astype(F32)
    kept_ref[...] = jnp.concatenate([own, part], axis=0)


def chunk_kernel(reps, kept_ref, *refs):
    got, (chunk_ref, parts_ref) = refs[: reps - 1], refs[reps - 1 :]
    depth = chunk_ref.shape[0]
    rows = kept_ref.shape[0] - depth
    rep = lax.axis_index("rep")
    parts_ref[rep] = kept_ref[rows:, :].astype(BF16).astype(F32)
    for step in range(1, reps):
        parts_ref[origin_of("D", rep, step, reps)] = got[step - 1][rows:, :].astype(F32)
    chunk = parts_ref[0]
    for other in range(1, reps):
        chunk += parts_ref[other]
    chunk_ref[...] = chunk.astype(BF16)


def grad_x_kernel(kept_ref, *refs):
    got, grad_x_ref = refs[:-1], refs[-1]
    rows = grad_x_ref.shape[0]
    total = kept_ref[:rows, :]
    for ref in got:
        total += ref[:rows, :].astype(F32)
    grad_x_ref[...] = total.astype(BF16)


def grad_w_kernel(scale, own_ref, mate_ref, grad_w_ref):
    part = own_ref.shape[0]
    core = lax.rem(lax.axis_index("rows"), PAIR)
    for half, ref in ((core, own_ref), (1 - core, mate_ref)):
        first = pl.multiple_of(half * part, part)
        grad_w_ref[pl.ds(first, part), :] = ref[...].astype(F32) * scale


def local(features, weight, tiles, send_src, send_dst, cotangent):
    blocks = tiles[0, 0]
    source = send_src[0, 0]
    target = send_dst[0, 0]
    peers, slot_count = target.shape
    rows, width = features.shape
    cols, per_col, block = blocks.shape[:3]
    reps = lax.axis_size("rep")
    chips = peers // PAIR
    slots = peers * PAD
    chunk = width // PAIR

    def over_rep(name, value, step):
        return lax.ppermute(value, "rep", list(enumerate(targets(name, step, reps))))

    def over_chips(name, value, step):
        pairs = [
            (i * PAIR + core, to * PAIR + core)
            for i, to in enumerate(targets(name, step, chips))
            for core in range(PAIR)
        ]
        return lax.ppermute(value, "rows", pairs)

    def to_mate(value):
        return lax.ppermute(value, "rows", [(i, i ^ 1) for i in range(peers)])

    gathered = [over_rep("A", features, step) for step in range(1, reps)]

    picked, base = pl.pallas_call(
        lambda *refs: inputs_kernel(chips, *refs),
        out_shape=(
            jax.ShapeDtypeStruct((cols, slots, block), BF16),
            jax.ShapeDtypeStruct((slots, width), F32),
        ),
        in_specs=whole(3) + [pl.BlockSpec(memory_space=pl.ANY)],
        out_specs=tuple(whole(2)),
        scratch_shapes=[
            pltpu.VMEM((cols, per_col, block, block), BF16),
            pltpu.VMEM((peers, LANES), jnp.int32),
            pltpu.SemaphoreType.DMA((cols,)),
        ],
        compiler_params=params(slots),
        name="inputs",
    )(source, target, features, blocks)

    message = jax.ShapeDtypeStruct((PAIR * PAD, width), BF16)
    outgoing = pl.pallas_call(
        lambda *refs: partial_kernel(reps, chips, *refs),
        out_shape=(message,) * chips,
        in_specs=whole(1 + reps),
        out_specs=tuple(whole(chips)),
        scratch_shapes=[pltpu.VMEM((slots, width), F32)],
        compiler_params=params(slots),
        name="partial",
    )(picked, base, *gathered)

    direct = [outgoing[0]] + [over_chips("B", outgoing[step], step) for step in range(1, chips)]
    shared = [to_mate(value) for value in direct]
    early_features, early_cotangent, _ = lax.optimization_barrier(
        (features, cotangent, outgoing[0])
    )

    output, back_in, *requested = pl.pallas_call(
        lambda *refs: layer_kernel(chips, slot_count, *refs),
        out_shape=(
            jax.ShapeDtypeStruct((rows, width), BF16),
            jax.ShapeDtypeStruct((rows, width), BF16),
        )
        + (jax.ShapeDtypeStruct((PAIR * PAD + chunk, width), BF16),) * chips,
        in_specs=whole(PAIR * chips + 5),
        out_specs=tuple(whole(2 + chips)),
        scratch_shapes=[pltpu.VMEM((width, width), F32)],
        compiler_params=params(slots),
        name="layer",
    )(
        *direct,
        *shared,
        features,
        to_mate(early_features),
        cotangent,
        to_mate(early_cotangent),
        weight,
    )

    returned = [requested[0]] + [over_chips("C", requested[step], step) for step in range(1, chips)]

    kept, *sends = pl.pallas_call(
        lambda *refs: terms_kernel(reps, chips, *refs),
        out_shape=(jax.ShapeDtypeStruct((rows + chunk, width), F32),)
        + (jax.ShapeDtypeStruct((rows + chunk, width), BF16),) * (reps - 1),
        in_specs=whole(2 + chips),
        out_specs=tuple(whole(reps)),
        scratch_shapes=[
            pltpu.VMEM((slots, width), BF16),
            pltpu.VMEM((chips, chunk, width), F32),
        ],
        compiler_params=params(slots),
        name="terms",
    )(picked, back_in, *returned)

    arrived = [over_rep("D", sends[step - 1], step) for step in range(1, reps)]

    share = pl.pallas_call(
        lambda *refs: chunk_kernel(reps, *refs),
        out_shape=jax.ShapeDtypeStruct((chunk, width), BF16),
        in_specs=whole(reps),
        out_specs=whole(1)[0],
        scratch_shapes=[pltpu.VMEM((reps, chunk, width), F32)],
        compiler_params=params(slots),
        name="chunk",
    )(kept, *arrived)

    grad_x = pl.pallas_call(
        grad_x_kernel,
        out_shape=jax.ShapeDtypeStruct((rows, width), BF16),
        in_specs=whole(reps),
        out_specs=whole(1)[0],
        compiler_params=params(slots),
        name="grad_x",
    )(kept, *arrived)

    node_count = rows * lax.axis_size("rows") * reps
    grad_w = pl.pallas_call(
        lambda *refs: grad_w_kernel(1.0 / math.sqrt(node_count), *refs),
        out_shape=jax.ShapeDtypeStruct((width, width), F32),
        in_specs=whole(2),
        out_specs=whole(1)[0],
        compiler_params=params(slots),
        name="grad_w",
    )(share, to_mate(share))
    return (output, grad_w, grad_x)


def solution(mesh):
    placed = (
        P(("rows", "rep"), None),
        P(),
        P("rows", "rep", None, None, None, None),
        P("rows", "rep", None, None),
        P("rows", "rep", None, None),
        P(("rows", "rep"), None),
    )
    return jax.shard_map(
        local,
        mesh=mesh,
        in_specs=placed,
        out_specs=(P(("rows", "rep"), None), P(), P(("rows", "rep"), None)),
        check_vma=False,
    )
```

```python
import math

import jax
import jax.numpy as jnp
from jax import lax
from jax.experimental import pallas as pl
from jax.experimental.pallas import tpu as pltpu
from jax.sharding import PartitionSpec as P

BF16 = jnp.bfloat16
F32 = jnp.float32
PAD = 32
LANES = 128
PAIR = 2
MOST_ROWS = 4096


def whole(count):
    return [pl.BlockSpec(memory_space=pltpu.VMEM)] * count


def params(slots):
    return pltpu.CompilerParams(vmem_limit_bytes=(4 << 20) + (16 << 10) * slots)


def dot(a, b, contract_a, contract_b):
    return lax.dot_general(
        a, b, (((contract_a,), (contract_b,)), ((), ())), preferred_element_type=F32
    )


LOW, HIGH, BOTH = (1, 0, 3, 2), (2, 3, 0, 1), (3, 2, 1, 0)
RING, REVERSE = (2, 3, 1, 0), (3, 2, 0, 1)
PLAN = dict(
    A=(LOW, BOTH, HIGH), B=(BOTH, LOW, HIGH), C=(LOW, HIGH, BOTH), D=(REVERSE, RING, LOW)
)


def targets(name, step, count):
    if step == 0:
        return tuple(range(count))
    if count == len(PLAN[name]) + 1:
        return PLAN[name][step - 1]
    return tuple((i + step) % count for i in range(count))


def entry(table, index):
    found = table[0]
    for i in range(1, len(table)):
        found = jnp.where(index == i, table[i], found)
    return found


def target_of(name, index, step, count):
    return entry(targets(name, step, count), index)


def origin_of(name, index, step, count):
    sent = targets(name, step, count)
    return entry(tuple(sent.index(i) for i in range(count)), index)


def step_to(name, index, other, count):
    found = jnp.zeros_like(other)
    for step in range(1, count):
        found = jnp.where(target_of(name, index, step, count) == other, step, found)
    return found


def asked_at(step, count):
    back = targets("C", step, count)
    for at in range(count):
        there = targets("B", at, count)
        if all(there[back[i]] == i for i in range(count)):
            return at
    raise ValueError("B and C differ")


def inputs_kernel(
    chips, plane, source_ref, target_ref, features_ref, tiles_ref, picked_ref, base_ref, named_ref
):
    cols, per_col, block = tiles_ref.shape[:3]
    peers, slot_count = source_ref.shape
    slots, width = base_ref.shape
    wide = width // PAD
    chip = lax.div(lax.axis_index("rows"), PAIR)
    target = target_ref[...]
    named_ref[...] = jnp.full(named_ref.shape, -1, jnp.int32)
    named_ref[:, :slot_count] = jnp.where(target < features_ref.shape[0], source_ref[...], -1)
    spread = jnp.broadcast_to(named_ref[...][:, None, :], (peers, PAD, LANES)).reshape(slots, LANES)
    slot = lax.rem(lax.broadcasted_iota(jnp.int32, (slots, LANES), 0), PAD)
    lane = lax.broadcasted_iota(jnp.int32, (slots, LANES), 1)
    column = jnp.sum(jnp.where(lane == slot, spread, 0).astype(F32), axis=1, keepdims=True)
    offset = jnp.broadcast_to(column, (slots, LANES)) - lane.astype(F32)

    named_ref[...] = jnp.zeros(named_ref.shape, jnp.int32)
    named_ref[:, :slot_count] = target
    notes = named_ref[...]
    tiled = notes
    for turn in range(1, LANES // PAD):
        tiled += pltpu.roll(notes, turn * PAD, 1)
    tiled = jnp.concatenate([tiled] * (width // LANES), axis=1)
    tiled = jnp.broadcast_to(tiled[:, None, :], (peers, PAD, width)).reshape(slots, width)
    row = lax.broadcasted_iota(jnp.int32, (slots, width), 0)
    if plane:
        keep = lax.rem(row, PAD) == slot_count
    else:
        spot = lax.div(lax.broadcasted_iota(jnp.int32, (slots, width), 1), PAD)
        at = step_to("B", chip, lax.div(row, PAD * PAIR), chips)
        keep = jnp.zeros((slots, width), jnp.bool_)
        for mate in range(PAIR):
            here = lax.rem(row, PAD) == slot_count + mate
            keep = keep | (here & (lax.rem(mate * chips + at, wide) == spot))
    landing = jnp.where(keep, tiled, 0).astype(F32)

    for b in range(cols):
        first = b * per_col
        hot = jnp.concatenate(
            [
                jnp.where(offset == float((first + k) * block), 1.0, 0.0).astype(BF16)
                for k in range(per_col)
            ],
            axis=1,
        )
        rows = tiles_ref[b].reshape(per_col * block, block)
        picked_ref[b] = dot(hot, rows, 1, 0).astype(BF16)
    base_ref[...] = landing + dot(picked_ref[lax.axis_index("rep")], features_ref[...], 1, 0)


def partial_kernel(reps, chips, picked_ref, base_ref, *refs):
    features, sends, total_ref = refs[: reps - 1], refs[reps - 1 : -1], refs[-1]
    rep = lax.axis_index("rep")
    chip = lax.div(lax.axis_index("rows"), PAIR)
    depth = PAIR * PAD
    total = base_ref[...]
    for step in range(1, reps):
        total += dot(picked_ref[origin_of("A", rep, step, reps)], features[step - 1][...], 1, 0)
    if len(sends) == 1:
        sends[0][...] = total.astype(BF16)
        return
    total_ref[...] = total
    for step in range(chips):
        first = pl.multiple_of(target_of("B", chip, step, chips) * depth, depth)
        sends[step][...] = total_ref[pl.ds(first, depth), :].astype(BF16)


def plane_kernel(reps, chips, slot_count, picked_ref, weight_ref, *refs):
    peers = PAIR * chips
    got, nodes, refs = refs[:peers], refs[peers : 2 * peers], refs[2 * peers :]
    output_ref, kept_ref, *sends, aggregated_ref, grads_ref, block_ref, rows_ref = refs
    rows, width = output_ref.shape
    wide = width // PAD
    rep = lax.axis_index("rep")
    core = lax.rem(lax.axis_index("rows"), PAIR)
    chip = lax.div(lax.axis_index("rows"), PAIR)
    groups = pl.cdiv(peers, wide)
    device = [
        origin_of("B", chip, at % chips, chips) * PAIR + (core if at < chips else 1 - core)
        for at in range(peers)
    ]
    row = lax.broadcasted_iota(jnp.int32, (rows, width), 0)
    lane = lax.broadcasted_iota(jnp.int32, (rows, width), 1)
    valid = lax.rem(lane, PAD) < slot_count
    spot = lax.div(lax.broadcasted_iota(jnp.int32, (1, width), 1), PAD)
    own_lanes = (lane < slot_count)[:, :LANES]
    weight = weight_ref[...]
    for at in range(peers):
        first = pl.multiple_of(device[at] * PAD, PAD)
        notes = [jnp.zeros((1, width), F32)] * groups
        mine = None
        for source in range(peers):
            block = got[source][pl.ds(first, PAD), :]
            block_ref[at, pl.ds(pl.multiple_of(device[source] * PAD, PAD), PAD), :] = block
            note = block[16:].astype(F32)[slot_count - 16 :][:1]
            mine = note if source == 0 else mine
            for e in range(groups):
                notes[e] = jnp.where(spot + e * wide == device[source], note, notes[e])
        parts = [
            jnp.where(valid & (note.astype(jnp.int32) == row), 1.0, 0.0).astype(BF16)
            for note in notes
        ]
        hot = parts[0] if groups == 1 else jnp.concatenate(parts, axis=1)
        arrived = dot(hot[:, : peers * PAD], block_ref[at], 1, 0)
        aggregated = (nodes[at][:rows, :].astype(F32) + arrived).astype(BF16)
        preact = dot(aggregated, weight, 1, 0)
        sigmoid = jax.nn.sigmoid(preact)
        pre_grad = (
            nodes[at][rows:, :].astype(F32) * sigmoid * (1.0 + preact * (1.0 - sigmoid))
        ).astype(BF16)
        node = pl.multiple_of(device[at] * rows, rows)
        aggregated_ref[pl.ds(node, rows), :] = aggregated
        grads_ref[pl.ds(node, rows), :] = pre_grad
        here = own_lanes & (mine.astype(jnp.int32)[:, :LANES] == row[:, :LANES])
        asked = dot(jnp.where(here, 1.0, 0.0).astype(BF16), pre_grad, 0, 0)
        rows_ref[pl.ds(first, PAD), :] = asked[:PAD].astype(BF16)
        if at == 0:
            output_ref[...] = (preact * sigmoid).astype(BF16)
            back_in = dot(pre_grad, weight, 1, 1).astype(BF16)
    part = width // PAIR
    columns = aggregated_ref[:, :part]
    for half in range(1, PAIR):
        columns = jnp.where(core == half, aggregated_ref[:, half * part : (half + 1) * part], columns)
    grad = dot(columns, grads_ref[...], 0, 0)
    back = dot(rows_ref[...], weight, 1, 1).astype(BF16)
    for step in range(1, reps):
        term = dot(picked_ref[target_of("D", rep, step, reps)], back, 0, 0)
        sends[step - 1][...] = jnp.concatenate([term, grad], axis=0).astype(BF16)
    own = dot(picked_ref[rep], back, 0, 0) + back_in.astype(F32)
    kept_ref[...] = jnp.concatenate([own, grad], axis=0)


def layer_kernel(chips, slot_count, *refs):
    got, refs = refs[: PAIR * chips], refs[PAIR * chips :]
    features_ref, mate_features_ref, cotangent_ref, mate_cotangent_ref, weight_ref = refs[:5]
    output_ref, back_ref, *sends, grad_ref = refs[5:]
    rows, width = features_ref.shape
    wide = width // PAD
    core = lax.rem(lax.axis_index("rows"), PAIR)
    groups = pl.cdiv(PAIR * chips, wide)
    row = lax.broadcasted_iota(jnp.int32, (rows, width), 0)
    lane = lax.broadcasted_iota(jnp.int32, (rows, width), 1)
    valid = lax.rem(lane, PAD) < slot_count
    weight = weight_ref[...]
    hots, aggregates = [], []
    for half, own in ((core, features_ref), (1 - core, mate_features_ref)):
        first = pl.multiple_of(half * PAD, PAD)
        blocks = [ref[pl.ds(first, PAD), :] for ref in got]
        notes = [jnp.zeros((1, width), F32)] * groups
        for at, block in enumerate(blocks):
            mate = at // chips
            notes[at // wide] += block[16:].astype(F32)[slot_count - 16 + mate :][:1]
        parts = [
            jnp.where(valid & (note.astype(jnp.int32) == row), 1.0, 0.0).astype(BF16)
            for note in notes
        ]
        hot = parts[0] if groups == 1 else jnp.concatenate(parts, axis=1)
        hot = hot[:, : PAIR * chips * PAD]
        arrived = dot(hot, jnp.concatenate(blocks, axis=0), 1, 0)
        hots.append(hot[:, : chips * PAD])
        aggregates.append((own[...].astype(F32) + arrived).astype(BF16))
    aggregated = jnp.concatenate(aggregates, axis=0)
    preact = dot(aggregated, weight, 1, 0)
    sigmoid = jax.nn.sigmoid(preact)
    output_ref[...] = (preact * sigmoid)[:rows].astype(BF16)
    cotangent = jnp.concatenate([cotangent_ref[...], mate_cotangent_ref[...]], axis=0)
    pre_grad = (cotangent.astype(F32) * sigmoid * (1.0 + preact * (1.0 - sigmoid))).astype(BF16)
    back_in = dot(pre_grad, weight, 1, 1).astype(BF16)
    back_ref[...] = back_in[:rows]
    grad_ref[...] = dot(aggregated, pre_grad, 0, 0)
    part = width // PAIR
    grad = grad_ref[pl.ds(pl.multiple_of(core * part, part), part), :].astype(BF16)
    asked = [dot(hot, back_in[h * rows : (h + 1) * rows], 0, 0) for h, hot in enumerate(hots)]
    for step in range(chips):
        first = asked_at(step, chips) * PAD
        from_own, from_mate = (part[first : first + PAD].astype(BF16) for part in asked)
        sends[step][pl.ds(pl.multiple_of(core * PAD, PAD), PAD), :] = from_own
        sends[step][pl.ds(pl.multiple_of((1 - core) * PAD, PAD), PAD), :] = from_mate
        sends[step][PAIR * PAD :, :] = grad


def terms_kernel(reps, chips, picked_ref, back_ref, *refs):
    returned, kept_ref, sends = refs[:chips], refs[chips], refs[chips + 1 : -2]
    rows_ref, parts_ref = refs[-2:]
    rep = lax.axis_index("rep")
    chip = lax.div(lax.axis_index("rows"), PAIR)
    depth = PAIR * PAD
    for step in range(chips):
        origin = origin_of("C", chip, step, chips)
        rows_ref[pl.ds(pl.multiple_of(origin * depth, depth), depth), :] = returned[step][:depth, :]
        parts_ref[origin] = returned[step][depth:, :].astype(F32)
    part = parts_ref[0]
    for other in range(1, chips):
        part += parts_ref[other]
    rows = rows_ref[...]
    for step in range(1, reps):
        term = dot(picked_ref[target_of("D", rep, step, reps)], rows, 0, 0)
        sends[step - 1][...] = jnp.concatenate([term, part], axis=0).astype(BF16)
    own = dot(picked_ref[rep], rows, 0, 0) + back_ref[...].astype(F32)
    kept_ref[...] = jnp.concatenate([own, part], axis=0)


def chunk_kernel(reps, kept_ref, *refs):
    got, (chunk_ref, parts_ref) = refs[: reps - 1], refs[reps - 1 :]
    depth = chunk_ref.shape[0]
    rows = kept_ref.shape[0] - depth
    rep = lax.axis_index("rep")
    parts_ref[rep] = kept_ref[rows:, :].astype(BF16).astype(F32)
    for step in range(1, reps):
        parts_ref[origin_of("D", rep, step, reps)] = got[step - 1][rows:, :].astype(F32)
    chunk = parts_ref[0]
    for other in range(1, reps):
        chunk += parts_ref[other]
    chunk_ref[...] = chunk.astype(BF16)


def grad_x_kernel(kept_ref, *refs):
    got, grad_x_ref = refs[:-1], refs[-1]
    rows = grad_x_ref.shape[0]
    total = kept_ref[:rows, :]
    for ref in got:
        total += ref[:rows, :].astype(F32)
    grad_x_ref[...] = total.astype(BF16)


def grad_w_kernel(scale, own_ref, mate_ref, grad_w_ref):
    part = own_ref.shape[0]
    core = lax.rem(lax.axis_index("rows"), PAIR)
    for half, ref in ((core, own_ref), (1 - core, mate_ref)):
        first = pl.multiple_of(half * part, part)
        grad_w_ref[pl.ds(first, part), :] = ref[...].astype(F32) * scale


def local(features, weight, tiles, send_src, send_dst, cotangent):
    blocks = tiles[0, 0]
    source = send_src[0, 0]
    target = send_dst[0, 0]
    peers, slot_count = target.shape
    rows, width = features.shape
    cols, per_col, block = blocks.shape[:3]
    reps = lax.axis_size("rep")
    chips = peers // PAIR
    slots = peers * PAD
    chunk = width // PAIR
    plane = peers * slots <= MOST_ROWS

    def over_rep(name, value, step):
        return lax.ppermute(value, "rep", list(enumerate(targets(name, step, reps))))

    def over_chips(name, value, step):
        pairs = [
            (i * PAIR + core, to * PAIR + core)
            for i, to in enumerate(targets(name, step, chips))
            for core in range(PAIR)
        ]
        return lax.ppermute(value, "rows", pairs)

    def to_mate(value):
        return lax.ppermute(value, "rows", [(i, i ^ 1) for i in range(peers)])

    gathered = [over_rep("A", features, step) for step in range(1, reps)]

    picked, base = pl.pallas_call(
        lambda *refs: inputs_kernel(chips, plane, *refs),
        out_shape=(
            jax.ShapeDtypeStruct((cols, slots, block), BF16),
            jax.ShapeDtypeStruct((slots, width), F32),
        ),
        in_specs=whole(4),
        out_specs=tuple(whole(2)),
        scratch_shapes=[
            pltpu.VMEM((peers, LANES), jnp.int32),
        ],
        compiler_params=params(slots),
        name="inputs",
    )(source, target, features, blocks)

    def partial(shape, count):
        return pl.pallas_call(
            lambda *refs: partial_kernel(reps, chips, *refs),
            out_shape=(jax.ShapeDtypeStruct(shape, BF16),) * count,
            in_specs=whole(1 + reps),
            out_specs=tuple(whole(count)),
            scratch_shapes=[pltpu.VMEM((slots, width), F32)],
            compiler_params=params(slots),
            name="partial",
        )(picked, base, *gathered)

    if plane:
        (outgoing,) = partial((slots, width), 1)
        both = jnp.concatenate([features, cotangent], axis=0)
        if chips == 4:
            low, high = (over_chips("B", both, step) for step in (2, 3))
            nodes = [both, over_chips("B", high, 2), low, high]
        else:
            nodes = [both] + [over_chips("B", both, step) for step in range(1, chips)]
        direct = [outgoing] + [over_chips("B", outgoing, step) for step in range(1, chips)]
        *late, _ = lax.optimization_barrier((*nodes, outgoing))
        hops = [to_mate(value) for value in late]
        if chips > 1:
            hops[0], hops[chips // 2], direct[1] = lax.optimization_barrier(
                (hops[0], hops[chips // 2], direct[1])
            )
        nodes += hops
        rows_in = direct + [to_mate(value) for value in direct]
        output, kept, *sends = pl.pallas_call(
            lambda *refs: plane_kernel(reps, chips, slot_count, *refs),
            out_shape=(
                jax.ShapeDtypeStruct((rows, width), BF16),
                jax.ShapeDtypeStruct((rows + chunk, width), F32),
            )
            + (jax.ShapeDtypeStruct((rows + chunk, width), BF16),) * (reps - 1),
            in_specs=whole(2 + 2 * peers),
            out_specs=tuple(whole(1 + reps)),
            scratch_shapes=[
                pltpu.VMEM((peers * rows, width), BF16),
                pltpu.VMEM((peers * rows, width), BF16),
                pltpu.VMEM((peers, slots, width), BF16),
                pltpu.VMEM((slots, width), BF16),
            ],
            compiler_params=params(slots),
            name="plane",
        )(picked, weight, *rows_in, *nodes)
    else:
        outgoing = partial((PAIR * PAD, width), chips)
        direct = [outgoing[0]] + [over_chips("B", outgoing[step], step) for step in range(1, chips)]
        shared = [to_mate(value) for value in direct]
        early_features, early_cotangent, _ = lax.optimization_barrier(
            (features, cotangent, outgoing[0])
        )

        output, back_in, *requested = pl.pallas_call(
            lambda *refs: layer_kernel(chips, slot_count, *refs),
            out_shape=(
                jax.ShapeDtypeStruct((rows, width), BF16),
                jax.ShapeDtypeStruct((rows, width), BF16),
            )
            + (jax.ShapeDtypeStruct((PAIR * PAD + chunk, width), BF16),) * chips,
            in_specs=whole(PAIR * chips + 5),
            out_specs=tuple(whole(2 + chips)),
            scratch_shapes=[pltpu.VMEM((width, width), F32)],
            compiler_params=params(slots),
            name="layer",
        )(
            *direct,
            *shared,
            features,
            to_mate(early_features),
            cotangent,
            to_mate(early_cotangent),
            weight,
        )

        returned = [requested[0]] + [over_chips("C", requested[step], step) for step in range(1, chips)]

        kept, *sends = pl.pallas_call(
            lambda *refs: terms_kernel(reps, chips, *refs),
            out_shape=(jax.ShapeDtypeStruct((rows + chunk, width), F32),)
            + (jax.ShapeDtypeStruct((rows + chunk, width), BF16),) * (reps - 1),
            in_specs=whole(2 + chips),
            out_specs=tuple(whole(reps)),
            scratch_shapes=[
                pltpu.VMEM((slots, width), BF16),
                pltpu.VMEM((chips, chunk, width), F32),
            ],
            compiler_params=params(slots),
            name="terms",
        )(picked, back_in, *returned)

    arrived = [over_rep("D", sends[step - 1], step) for step in range(1, reps)]

    share = pl.pallas_call(
        lambda *refs: chunk_kernel(reps, *refs),
        out_shape=jax.ShapeDtypeStruct((chunk, width), BF16),
        in_specs=whole(reps),
        out_specs=whole(1)[0],
        scratch_shapes=[pltpu.VMEM((reps, chunk, width), F32)],
        compiler_params=params(slots),
        name="chunk",
    )(kept, *arrived)

    grad_x = pl.pallas_call(
        grad_x_kernel,
        out_shape=jax.ShapeDtypeStruct((rows, width), BF16),
        in_specs=whole(reps),
        out_specs=whole(1)[0],
        compiler_params=params(slots),
        name="grad_x",
    )(kept, *arrived)

    node_count = rows * lax.axis_size("rows") * reps
    grad_w = pl.pallas_call(
        lambda *refs: grad_w_kernel(1.0 / math.sqrt(node_count), *refs),
        out_shape=jax.ShapeDtypeStruct((width, width), F32),
        in_specs=whole(2),
        out_specs=whole(1)[0],
        compiler_params=params(slots),
        name="grad_w",
    )(share, to_mate(share))
    return (output, grad_w, grad_x)


def solution(mesh):
    placed = (
        P(("rows", "rep"), None),
        P(),
        P("rows", "rep", None, None, None, None),
        P("rows", "rep", None, None),
        P("rows", "rep", None, None),
        P(("rows", "rep"), None),
    )
    return jax.shard_map(
        local,
        mesh=mesh,
        in_specs=placed,
        out_specs=(P(("rows", "rep"), None), P(), P(("rows", "rep"), None)),
        check_vma=False,
    )
```

```python
import math

import jax
import jax.numpy as jnp
from jax import lax
from jax.experimental import pallas as pl
from jax.experimental.pallas import tpu as pltpu
from jax.sharding import PartitionSpec as P

BF16 = jnp.bfloat16
F32 = jnp.float32
PAD = 32
LANES = 128
PAIR = 2
MOST_ROWS = 4096


def whole(count):
    return [pl.BlockSpec(memory_space=pltpu.VMEM)] * count


def params(slots):
    return pltpu.CompilerParams(vmem_limit_bytes=(4 << 20) + (16 << 10) * slots)


def dot(a, b, contract_a, contract_b):
    return lax.dot_general(
        a, b, (((contract_a,), (contract_b,)), ((), ())), preferred_element_type=F32
    )


LOW, HIGH, BOTH = (1, 0, 3, 2), (2, 3, 0, 1), (3, 2, 1, 0)
RING, REVERSE = (2, 3, 1, 0), (3, 2, 0, 1)
PLAN = dict(
    A=(LOW, BOTH, HIGH), B=(BOTH, LOW, HIGH), C=(LOW, HIGH, BOTH), D=(REVERSE, RING, LOW)
)


def targets(name, step, count):
    if step == 0:
        return tuple(range(count))
    if count == len(PLAN[name]) + 1:
        return PLAN[name][step - 1]
    return tuple((i + step) % count for i in range(count))


def entry(table, index):
    found = table[0]
    for i in range(1, len(table)):
        found = jnp.where(index == i, table[i], found)
    return found


def target_of(name, index, step, count):
    return entry(targets(name, step, count), index)


def origin_of(name, index, step, count):
    sent = targets(name, step, count)
    return entry(tuple(sent.index(i) for i in range(count)), index)


def step_to(name, index, other, count):
    found = jnp.zeros_like(other)
    for step in range(1, count):
        found = jnp.where(target_of(name, index, step, count) == other, step, found)
    return found


def asked_at(step, count):
    back = targets("C", step, count)
    for at in range(count):
        there = targets("B", at, count)
        if all(there[back[i]] == i for i in range(count)):
            return at
    raise ValueError("B and C differ")


def inputs_kernel(
    chips, plane, source_ref, target_ref, features_ref, tiles_ref, picked_ref, base_ref, wanted_ref, named_ref
):
    cols, per_col, block = tiles_ref.shape[:3]
    peers, slot_count = source_ref.shape
    slots, width = base_ref.shape
    wide = width // PAD
    chip = lax.div(lax.axis_index("rows"), PAIR)
    target = target_ref[...]
    named_ref[...] = jnp.full(named_ref.shape, -1, jnp.int32)
    named_ref[:, :slot_count] = jnp.where(target < features_ref.shape[0], source_ref[...], -1)
    spread = jnp.broadcast_to(named_ref[...][:, None, :], (peers, PAD, LANES)).reshape(slots, LANES)
    slot = lax.rem(lax.broadcasted_iota(jnp.int32, (slots, LANES), 0), PAD)
    lane = lax.broadcasted_iota(jnp.int32, (slots, LANES), 1)
    column = jnp.sum(jnp.where(lane == slot, spread, 0).astype(F32), axis=1, keepdims=True)
    offset = jnp.broadcast_to(column, (slots, LANES)) - lane.astype(F32)

    named_ref[...] = jnp.zeros(named_ref.shape, jnp.int32)
    named_ref[:, :slot_count] = target
    notes = named_ref[...]
    spread = jnp.broadcast_to(notes[:, None, :], (peers, PAD, LANES)).reshape(slots, LANES)
    landing = jnp.sum(jnp.where(lane == slot, spread, 0).astype(F32), axis=1, keepdims=True)
    here = (jnp.broadcast_to(landing, (slots, LANES)) == lane.astype(F32)) & (slot < slot_count)
    wanted_ref[...] = jnp.where(here, 1.0, 0.0).astype(BF16)
    tiled = notes
    for turn in range(1, LANES // PAD):
        tiled += pltpu.roll(notes, turn * PAD, 1)
    tiled = jnp.concatenate([tiled] * (width // LANES), axis=1)
    tiled = jnp.broadcast_to(tiled[:, None, :], (peers, PAD, width)).reshape(slots, width)
    row = lax.broadcasted_iota(jnp.int32, (slots, width), 0)
    if plane:
        keep = lax.rem(row, PAD) == slot_count
    else:
        spot = lax.div(lax.broadcasted_iota(jnp.int32, (slots, width), 1), PAD)
        at = step_to("B", chip, lax.div(row, PAD * PAIR), chips)
        keep = jnp.zeros((slots, width), jnp.bool_)
        for mate in range(PAIR):
            here = lax.rem(row, PAD) == slot_count + mate
            keep = keep | (here & (lax.rem(mate * chips + at, wide) == spot))
    landing = jnp.where(keep, tiled, 0).astype(F32)

    for b in range(cols):
        first = b * per_col
        hot = jnp.concatenate(
            [
                jnp.where(offset == float((first + k) * block), 1.0, 0.0).astype(BF16)
                for k in range(per_col)
            ],
            axis=1,
        )
        rows = tiles_ref[b].reshape(per_col * block, block)
        picked_ref[b] = dot(hot, rows, 1, 0).astype(BF16)
    base_ref[...] = landing + dot(picked_ref[lax.axis_index("rep")], features_ref[...], 1, 0)


def partial_kernel(reps, chips, picked_ref, base_ref, *refs):
    features, sends, total_ref = refs[: reps - 1], refs[reps - 1 : -1], refs[-1]
    rep = lax.axis_index("rep")
    chip = lax.div(lax.axis_index("rows"), PAIR)
    depth = PAIR * PAD
    total = base_ref[...]
    for step in range(1, reps):
        total += dot(picked_ref[origin_of("A", rep, step, reps)], features[step - 1][...], 1, 0)
    if len(sends) == 1:
        sends[0][...] = total.astype(BF16)
        return
    total_ref[...] = total
    for step in range(chips):
        first = pl.multiple_of(target_of("B", chip, step, chips) * depth, depth)
        sends[step][...] = total_ref[pl.ds(first, depth), :].astype(BF16)


def plane_kernel(reps, chips, slot_count, picked_ref, wanted_ref, weight_ref, *refs):
    peers = PAIR * chips
    got, nodes, refs = refs[:peers], refs[peers : 2 * peers], refs[2 * peers :]
    output_ref, kept_ref, *sends, aggregated_ref, cotangent_ref, block_ref, wide_ref = refs
    rows, width = output_ref.shape
    wide = width // PAD
    rep = lax.axis_index("rep")
    core = lax.rem(lax.axis_index("rows"), PAIR)
    chip = lax.div(lax.axis_index("rows"), PAIR)
    groups = pl.cdiv(peers, wide)
    wide_ref[...] = jnp.zeros(wide_ref.shape, BF16)
    for at in range(peers):
        here = slice(at * PAD, (at + 1) * PAD)
        wide_ref[here, at * rows : (at + 1) * rows] = wanted_ref[here, :]
    device = [
        origin_of("B", chip, at % chips, chips) * PAIR + (core if at < chips else 1 - core)
        for at in range(peers)
    ]
    row = lax.broadcasted_iota(jnp.int32, (rows, width), 0)
    lane = lax.broadcasted_iota(jnp.int32, (rows, width), 1)
    valid = lax.rem(lane, PAD) < slot_count
    spot = lax.div(lax.broadcasted_iota(jnp.int32, (1, width), 1), PAD)
    weight = weight_ref[...]
    hots = []
    for at in range(peers):
        first = pl.multiple_of(device[at] * PAD, PAD)
        notes = [jnp.zeros((1, width), F32)] * groups
        for source in range(peers):
            block = got[source][pl.ds(first, PAD), :]
            block_ref[at, pl.ds(pl.multiple_of(device[source] * PAD, PAD), PAD), :] = block
            note = block[16:].astype(F32)[slot_count - 16 :][:1]
            for e in range(groups):
                notes[e] = jnp.where(spot + e * wide == device[source], note, notes[e])
        parts = [
            jnp.where(valid & (note.astype(jnp.int32) == row), 1.0, 0.0).astype(BF16)
            for note in notes
        ]
        hot = parts[0] if groups == 1 else jnp.concatenate(parts, axis=1)
        hots.append(hot[:, : peers * PAD])
    arrived = [dot(hots[at], block_ref[at], 1, 0) for at in range(peers)]
    aggregates = [
        (nodes[at][:rows, :].astype(F32) + arrived[at]).astype(BF16) for at in range(peers)
    ]
    for at in range(peers):
        node = pl.multiple_of(device[at] * rows, rows)
        aggregated_ref[pl.ds(node, rows), :] = aggregates[at]
        cotangent_ref[pl.ds(node, rows), :] = nodes[at][rows:, :]

    def layer(aggregated, cotangent):
        preact = dot(aggregated, weight, 1, 0)
        sigmoid = jax.nn.sigmoid(preact)
        pre_grad = cotangent.astype(F32) * sigmoid * (1.0 + preact * (1.0 - sigmoid))
        return (preact * sigmoid).astype(BF16), pre_grad.astype(BF16)

    output_ref[...], own_grad = layer(aggregates[0], nodes[0][rows:, :])
    back_in = dot(own_grad, weight, 1, 1).astype(BF16)
    _, grads = layer(aggregated_ref[...], cotangent_ref[...])
    part = width // PAIR
    columns = aggregated_ref[:, :part]
    for half in range(1, PAIR):
        columns = jnp.where(core == half, aggregated_ref[:, half * part : (half + 1) * part], columns)
    grad = dot(columns, grads, 0, 0)
    asked = dot(wide_ref[...], grads, 1, 0).astype(BF16)
    back = dot(asked, weight, 1, 1).astype(BF16)
    for step in range(1, reps):
        term = dot(picked_ref[target_of("D", rep, step, reps)], back, 0, 0)
        sends[step - 1][...] = jnp.concatenate([term, grad], axis=0).astype(BF16)
    own = dot(picked_ref[rep], back, 0, 0) + back_in.astype(F32)
    kept_ref[...] = jnp.concatenate([own, grad], axis=0)


def layer_kernel(chips, slot_count, *refs):
    got, refs = refs[: PAIR * chips], refs[PAIR * chips :]
    features_ref, mate_features_ref, cotangent_ref, mate_cotangent_ref, weight_ref = refs[:5]
    output_ref, back_ref, *sends, grad_ref = refs[5:]
    rows, width = features_ref.shape
    wide = width // PAD
    core = lax.rem(lax.axis_index("rows"), PAIR)
    groups = pl.cdiv(PAIR * chips, wide)
    row = lax.broadcasted_iota(jnp.int32, (rows, width), 0)
    lane = lax.broadcasted_iota(jnp.int32, (rows, width), 1)
    valid = lax.rem(lane, PAD) < slot_count
    weight = weight_ref[...]
    hots, aggregates = [], []
    for half, own in ((core, features_ref), (1 - core, mate_features_ref)):
        first = pl.multiple_of(half * PAD, PAD)
        blocks = [ref[pl.ds(first, PAD), :] for ref in got]
        notes = [jnp.zeros((1, width), F32)] * groups
        for at, block in enumerate(blocks):
            mate = at // chips
            notes[at // wide] += block[16:].astype(F32)[slot_count - 16 + mate :][:1]
        parts = [
            jnp.where(valid & (note.astype(jnp.int32) == row), 1.0, 0.0).astype(BF16)
            for note in notes
        ]
        hot = parts[0] if groups == 1 else jnp.concatenate(parts, axis=1)
        hot = hot[:, : PAIR * chips * PAD]
        arrived = dot(hot, jnp.concatenate(blocks, axis=0), 1, 0)
        hots.append(hot[:, : chips * PAD])
        aggregates.append((own[...].astype(F32) + arrived).astype(BF16))
    aggregated = jnp.concatenate(aggregates, axis=0)
    preact = dot(aggregated, weight, 1, 0)
    sigmoid = jax.nn.sigmoid(preact)
    output_ref[...] = (preact * sigmoid)[:rows].astype(BF16)
    cotangent = jnp.concatenate([cotangent_ref[...], mate_cotangent_ref[...]], axis=0)
    pre_grad = (cotangent.astype(F32) * sigmoid * (1.0 + preact * (1.0 - sigmoid))).astype(BF16)
    back_in = dot(pre_grad, weight, 1, 1).astype(BF16)
    back_ref[...] = back_in[:rows]
    grad_ref[...] = dot(aggregated, pre_grad, 0, 0)
    part = width // PAIR
    grad = grad_ref[pl.ds(pl.multiple_of(core * part, part), part), :].astype(BF16)
    asked = [dot(hot, back_in[h * rows : (h + 1) * rows], 0, 0) for h, hot in enumerate(hots)]
    for step in range(chips):
        first = asked_at(step, chips) * PAD
        from_own, from_mate = (part[first : first + PAD].astype(BF16) for part in asked)
        sends[step][pl.ds(pl.multiple_of(core * PAD, PAD), PAD), :] = from_own
        sends[step][pl.ds(pl.multiple_of((1 - core) * PAD, PAD), PAD), :] = from_mate
        sends[step][PAIR * PAD :, :] = grad


def terms_kernel(reps, chips, picked_ref, back_ref, *refs):
    returned, kept_ref, sends = refs[:chips], refs[chips], refs[chips + 1 : -2]
    rows_ref, parts_ref = refs[-2:]
    rep = lax.axis_index("rep")
    chip = lax.div(lax.axis_index("rows"), PAIR)
    depth = PAIR * PAD
    for step in range(chips):
        origin = origin_of("C", chip, step, chips)
        rows_ref[pl.ds(pl.multiple_of(origin * depth, depth), depth), :] = returned[step][:depth, :]
        parts_ref[origin] = returned[step][depth:, :].astype(F32)
    part = parts_ref[0]
    for other in range(1, chips):
        part += parts_ref[other]
    rows = rows_ref[...]
    for step in range(1, reps):
        term = dot(picked_ref[target_of("D", rep, step, reps)], rows, 0, 0)
        sends[step - 1][...] = jnp.concatenate([term, part], axis=0).astype(BF16)
    own = dot(picked_ref[rep], rows, 0, 0) + back_ref[...].astype(F32)
    kept_ref[...] = jnp.concatenate([own, part], axis=0)


def chunk_kernel(reps, kept_ref, *refs):
    got, (chunk_ref, parts_ref) = refs[: reps - 1], refs[reps - 1 :]
    depth = chunk_ref.shape[0]
    rows = kept_ref.shape[0] - depth
    rep = lax.axis_index("rep")
    parts_ref[rep] = kept_ref[rows:, :].astype(BF16).astype(F32)
    for step in range(1, reps):
        parts_ref[origin_of("D", rep, step, reps)] = got[step - 1][rows:, :].astype(F32)
    chunk = parts_ref[0]
    for other in range(1, reps):
        chunk += parts_ref[other]
    chunk_ref[...] = chunk.astype(BF16)


def grad_x_kernel(kept_ref, *refs):
    got, grad_x_ref = refs[:-1], refs[-1]
    rows = grad_x_ref.shape[0]
    total = kept_ref[:rows, :]
    for ref in got:
        total += ref[:rows, :].astype(F32)
    grad_x_ref[...] = total.astype(BF16)


def grad_w_kernel(scale, own_ref, mate_ref, grad_w_ref):
    part = own_ref.shape[0]
    core = lax.rem(lax.axis_index("rows"), PAIR)
    for half, ref in ((core, own_ref), (1 - core, mate_ref)):
        first = pl.multiple_of(half * part, part)
        grad_w_ref[pl.ds(first, part), :] = ref[...].astype(F32) * scale


def local(features, weight, tiles, send_src, send_dst, cotangent):
    blocks = tiles[0, 0]
    source = send_src[0, 0]
    target = send_dst[0, 0]
    peers, slot_count = target.shape
    rows, width = features.shape
    cols, per_col, block = blocks.shape[:3]
    reps = lax.axis_size("rep")
    chips = peers // PAIR
    slots = peers * PAD
    chunk = width // PAIR
    plane = peers * slots <= MOST_ROWS

    def over_rep(name, value, step):
        return lax.ppermute(value, "rep", list(enumerate(targets(name, step, reps))))

    def over_chips(name, value, step):
        pairs = [
            (i * PAIR + core, to * PAIR + core)
            for i, to in enumerate(targets(name, step, chips))
            for core in range(PAIR)
        ]
        return lax.ppermute(value, "rows", pairs)

    def to_mate(value):
        return lax.ppermute(value, "rows", [(i, i ^ 1) for i in range(peers)])

    gathered = [over_rep("A", features, step) for step in range(1, reps)]

    picked, base, wanted = pl.pallas_call(
        lambda *refs: inputs_kernel(chips, plane, *refs),
        out_shape=(
            jax.ShapeDtypeStruct((cols, slots, block), BF16),
            jax.ShapeDtypeStruct((slots, width), F32),
            jax.ShapeDtypeStruct((slots, rows), BF16),
        ),
        in_specs=whole(4),
        out_specs=tuple(whole(3)),
        scratch_shapes=[
            pltpu.VMEM((peers, LANES), jnp.int32),
        ],
        compiler_params=params(slots),
        name="inputs",
    )(source, target, features, blocks)

    def partial(shape, count):
        return pl.pallas_call(
            lambda *refs: partial_kernel(reps, chips, *refs),
            out_shape=(jax.ShapeDtypeStruct(shape, BF16),) * count,
            in_specs=whole(1 + reps),
            out_specs=tuple(whole(count)),
            scratch_shapes=[pltpu.VMEM((slots, width), F32)],
            compiler_params=params(slots),
            name="partial",
        )(picked, base, *gathered)

    if plane:
        (outgoing,) = partial((slots, width), 1)
        both = jnp.concatenate([features, cotangent], axis=0)
        if chips == 4:
            low, high = (over_chips("B", both, step) for step in (2, 3))
            nodes = [both, over_chips("B", low, 3), low, high]
        else:
            nodes = [both] + [over_chips("B", both, step) for step in range(1, chips)]
        direct = [outgoing] + [over_chips("B", outgoing, step) for step in range(1, chips)]
        *late, _ = lax.optimization_barrier((*nodes, outgoing))
        hops = [to_mate(value) for value in late]
        if chips > 1:
            hops[0], hops[chips // 2], direct[1] = lax.optimization_barrier(
                (hops[0], hops[chips // 2], direct[1])
            )
        nodes += hops
        rows_in = direct + [to_mate(value) for value in direct]
        output, kept, *sends = pl.pallas_call(
            lambda *refs: plane_kernel(reps, chips, slot_count, *refs),
            out_shape=(
                jax.ShapeDtypeStruct((rows, width), BF16),
                jax.ShapeDtypeStruct((rows + chunk, width), F32),
            )
            + (jax.ShapeDtypeStruct((rows + chunk, width), BF16),) * (reps - 1),
            in_specs=whole(3 + 2 * peers),
            out_specs=tuple(whole(1 + reps)),
            scratch_shapes=[
                pltpu.VMEM((peers * rows, width), BF16),
                pltpu.VMEM((peers * rows, width), BF16),
                pltpu.VMEM((peers, slots, width), BF16),
                pltpu.VMEM((slots, peers * rows), BF16),
            ],
            compiler_params=params(slots),
            name="plane",
        )(picked, wanted, weight, *rows_in, *nodes)
    else:
        outgoing = partial((PAIR * PAD, width), chips)
        direct = [outgoing[0]] + [over_chips("B", outgoing[step], step) for step in range(1, chips)]
        shared = [to_mate(value) for value in direct]
        early_features, early_cotangent, _ = lax.optimization_barrier(
            (features, cotangent, outgoing[0])
        )

        output, back_in, *requested = pl.pallas_call(
            lambda *refs: layer_kernel(chips, slot_count, *refs),
            out_shape=(
                jax.ShapeDtypeStruct((rows, width), BF16),
                jax.ShapeDtypeStruct((rows, width), BF16),
            )
            + (jax.ShapeDtypeStruct((PAIR * PAD + chunk, width), BF16),) * chips,
            in_specs=whole(PAIR * chips + 5),
            out_specs=tuple(whole(2 + chips)),
            scratch_shapes=[pltpu.VMEM((width, width), F32)],
            compiler_params=params(slots),
            name="layer",
        )(
            *direct,
            *shared,
            features,
            to_mate(early_features),
            cotangent,
            to_mate(early_cotangent),
            weight,
        )

        returned = [requested[0]] + [over_chips("C", requested[step], step) for step in range(1, chips)]

        kept, *sends = pl.pallas_call(
            lambda *refs: terms_kernel(reps, chips, *refs),
            out_shape=(jax.ShapeDtypeStruct((rows + chunk, width), F32),)
            + (jax.ShapeDtypeStruct((rows + chunk, width), BF16),) * (reps - 1),
            in_specs=whole(2 + chips),
            out_specs=tuple(whole(reps)),
            scratch_shapes=[
                pltpu.VMEM((slots, width), BF16),
                pltpu.VMEM((chips, chunk, width), F32),
            ],
            compiler_params=params(slots),
            name="terms",
        )(picked, back_in, *returned)

    arrived = [over_rep("D", sends[step - 1], step) for step in range(1, reps)]

    share = pl.pallas_call(
        lambda *refs: chunk_kernel(reps, *refs),
        out_shape=jax.ShapeDtypeStruct((chunk, width), BF16),
        in_specs=whole(reps),
        out_specs=whole(1)[0],
        scratch_shapes=[pltpu.VMEM((reps, chunk, width), F32)],
        compiler_params=params(slots),
        name="chunk",
    )(kept, *arrived)

    grad_x = pl.pallas_call(
        grad_x_kernel,
        out_shape=jax.ShapeDtypeStruct((rows, width), BF16),
        in_specs=whole(reps),
        out_specs=whole(1)[0],
        compiler_params=params(slots),
        name="grad_x",
    )(kept, *arrived)

    node_count = rows * lax.axis_size("rows") * reps
    grad_w = pl.pallas_call(
        lambda *refs: grad_w_kernel(1.0 / math.sqrt(node_count), *refs),
        out_shape=jax.ShapeDtypeStruct((width, width), F32),
        in_specs=whole(2),
        out_specs=whole(1)[0],
        compiler_params=params(slots),
        name="grad_w",
    )(share, to_mate(share))
    return (output, grad_w, grad_x)


def solution(mesh):
    placed = (
        P(("rows", "rep"), None),
        P(),
        P("rows", "rep", None, None, None, None),
        P("rows", "rep", None, None),
        P("rows", "rep", None, None),
        P(("rows", "rep"), None),
    )
    return jax.shard_map(
        local,
        mesh=mesh,
        in_specs=placed,
        out_specs=(P(("rows", "rep"), None), P(), P(("rows", "rep"), None)),
        check_vma=False,
    )
```

```python
import math

import jax
import jax.numpy as jnp
from jax import lax
from jax.experimental import pallas as pl
from jax.experimental.pallas import tpu as pltpu
from jax.sharding import PartitionSpec as P

BF16 = jnp.bfloat16
F32 = jnp.float32
PAD = 32
LANES = 128
PAIR = 2
MOST_ROWS = 4096


def whole(count):
    return [pl.BlockSpec(memory_space=pltpu.VMEM)] * count


def params(slots):
    return pltpu.CompilerParams(vmem_limit_bytes=(4 << 20) + (16 << 10) * slots)


def dot(a, b, contract_a, contract_b):
    return lax.dot_general(
        a, b, (((contract_a,), (contract_b,)), ((), ())), preferred_element_type=F32
    )


LOW, HIGH, BOTH = (1, 0, 3, 2), (2, 3, 0, 1), (3, 2, 1, 0)
RING, REVERSE = (2, 3, 1, 0), (3, 2, 0, 1)
PLAN = dict(
    A=(LOW, BOTH, HIGH), B=(BOTH, LOW, HIGH), C=(LOW, HIGH, BOTH), D=(REVERSE, RING, LOW)
)


def targets(name, step, count):
    if step == 0:
        return tuple(range(count))
    if count == len(PLAN[name]) + 1:
        return PLAN[name][step - 1]
    return tuple((i + step) % count for i in range(count))


def entry(table, index):
    found = table[0]
    for i in range(1, len(table)):
        found = jnp.where(index == i, table[i], found)
    return found


def target_of(name, index, step, count):
    return entry(targets(name, step, count), index)


def origin_of(name, index, step, count):
    sent = targets(name, step, count)
    return entry(tuple(sent.index(i) for i in range(count)), index)


def step_to(name, index, other, count):
    found = jnp.zeros_like(other)
    for step in range(1, count):
        found = jnp.where(target_of(name, index, step, count) == other, step, found)
    return found


def asked_at(step, count):
    back = targets("C", step, count)
    for at in range(count):
        there = targets("B", at, count)
        if all(there[back[i]] == i for i in range(count)):
            return at
    raise ValueError("B and C differ")


def inputs_kernel(
    chips, plane, source_ref, target_ref, features_ref, tiles_ref, picked_ref, base_ref, wanted_ref, named_ref
):
    cols, per_col, block = tiles_ref.shape[:3]
    peers, slot_count = source_ref.shape
    slots, width = base_ref.shape
    wide = width // PAD
    chip = lax.div(lax.axis_index("rows"), PAIR)
    target = target_ref[...]
    named_ref[...] = jnp.full(named_ref.shape, -1, jnp.int32)
    named_ref[:, :slot_count] = jnp.where(target < features_ref.shape[0], source_ref[...], -1)
    spread = jnp.broadcast_to(named_ref[...][:, None, :], (peers, PAD, LANES)).reshape(slots, LANES)
    slot = lax.rem(lax.broadcasted_iota(jnp.int32, (slots, LANES), 0), PAD)
    lane = lax.broadcasted_iota(jnp.int32, (slots, LANES), 1)
    column = jnp.sum(jnp.where(lane == slot, spread, 0).astype(F32), axis=1, keepdims=True)
    offset = jnp.broadcast_to(column, (slots, LANES)) - lane.astype(F32)

    named_ref[...] = jnp.zeros(named_ref.shape, jnp.int32)
    named_ref[:, :slot_count] = target
    notes = named_ref[...]
    spread = jnp.broadcast_to(notes[:, None, :], (peers, PAD, LANES)).reshape(slots, LANES)
    landing = jnp.sum(jnp.where(lane == slot, spread, 0).astype(F32), axis=1, keepdims=True)
    here = (jnp.broadcast_to(landing, (slots, LANES)) == lane.astype(F32)) & (slot < slot_count)
    wanted_ref[...] = jnp.where(here, 1.0, 0.0).astype(BF16)
    tiled = notes
    for turn in range(1, LANES // PAD):
        tiled += pltpu.roll(notes, turn * PAD, 1)
    tiled = jnp.concatenate([tiled] * (width // LANES), axis=1)
    tiled = jnp.broadcast_to(tiled[:, None, :], (peers, PAD, width)).reshape(slots, width)
    row = lax.broadcasted_iota(jnp.int32, (slots, width), 0)
    if plane:
        keep = lax.rem(row, PAD) == slot_count
    else:
        spot = lax.div(lax.broadcasted_iota(jnp.int32, (slots, width), 1), PAD)
        at = step_to("B", chip, lax.div(row, PAD * PAIR), chips)
        keep = jnp.zeros((slots, width), jnp.bool_)
        for mate in range(PAIR):
            here = lax.rem(row, PAD) == slot_count + mate
            keep = keep | (here & (lax.rem(mate * chips + at, wide) == spot))
    landing = jnp.where(keep, tiled, 0).astype(F32)

    for b in range(cols):
        first = b * per_col
        hot = jnp.concatenate(
            [
                jnp.where(offset == float((first + k) * block), 1.0, 0.0).astype(BF16)
                for k in range(per_col)
            ],
            axis=1,
        )
        rows = tiles_ref[b].reshape(per_col * block, block)
        picked_ref[b] = dot(hot, rows, 1, 0).astype(BF16)
    base_ref[...] = landing + dot(picked_ref[lax.axis_index("rep")], features_ref[...], 1, 0)


def partial_kernel(reps, chips, picked_ref, base_ref, *refs):
    features, sends, total_ref = refs[: reps - 1], refs[reps - 1 : -1], refs[-1]
    rep = lax.axis_index("rep")
    chip = lax.div(lax.axis_index("rows"), PAIR)
    depth = PAIR * PAD
    total = base_ref[...]
    for step in range(1, reps):
        total += dot(picked_ref[origin_of("A", rep, step, reps)], features[step - 1][...], 1, 0)
    if len(sends) == 1:
        sends[0][...] = total.astype(BF16)
        return
    total_ref[...] = total
    for step in range(chips):
        first = pl.multiple_of(target_of("B", chip, step, chips) * depth, depth)
        sends[step][...] = total_ref[pl.ds(first, depth), :].astype(BF16)


def plane_kernel(reps, chips, slot_count, picked_ref, wanted_ref, weight_ref, *refs):
    peers = PAIR * chips
    got, nodes, refs = refs[:peers], refs[peers : 2 * peers], refs[2 * peers :]
    output_ref, kept_ref, *sends, aggregated_ref, cotangent_ref, block_ref, wide_ref = refs
    rows, width = output_ref.shape
    wide = width // PAD
    rep = lax.axis_index("rep")
    core = lax.rem(lax.axis_index("rows"), PAIR)
    chip = lax.div(lax.axis_index("rows"), PAIR)
    groups = pl.cdiv(peers, wide)
    wide_ref[...] = jnp.zeros(wide_ref.shape, BF16)
    for at in range(peers):
        here = slice(at * PAD, (at + 1) * PAD)
        wide_ref[here, at * rows : (at + 1) * rows] = wanted_ref[here, :]
    device = [
        origin_of("B", chip, at % chips, chips) * PAIR + (core if at < chips else 1 - core)
        for at in range(peers)
    ]
    row = lax.broadcasted_iota(jnp.int32, (rows, width), 0)
    lane = lax.broadcasted_iota(jnp.int32, (rows, width), 1)
    valid = lax.rem(lane, PAD) < slot_count
    spot = lax.div(lax.broadcasted_iota(jnp.int32, (1, width), 1), PAD)
    weight = weight_ref[...]
    hots = []
    for at in range(peers):
        first = pl.multiple_of(device[at] * PAD, PAD)
        notes = [jnp.zeros((1, width), F32)] * groups
        for source in range(peers):
            block = got[source][pl.ds(first, PAD), :]
            block_ref[at, pl.ds(pl.multiple_of(device[source] * PAD, PAD), PAD), :] = block
            note = block[16:].astype(F32)[slot_count - 16 :][:1]
            for e in range(groups):
                notes[e] = jnp.where(spot + e * wide == device[source], note, notes[e])
        parts = [
            jnp.where(valid & (note.astype(jnp.int32) == row), 1.0, 0.0).astype(BF16)
            for note in notes
        ]
        hot = parts[0] if groups == 1 else jnp.concatenate(parts, axis=1)
        hots.append(hot[:, : peers * PAD])
    arrived = [dot(hots[at], block_ref[at], 1, 0) for at in range(peers)]
    aggregates = [
        (nodes[at][:rows, :].astype(F32) + arrived[at]).astype(BF16) for at in range(peers)
    ]
    for at in range(peers):
        node = pl.multiple_of(device[at] * rows, rows)
        aggregated_ref[pl.ds(node, rows), :] = aggregates[at]
        cotangent_ref[pl.ds(node, rows), :] = nodes[at][rows:, :]

    def layer(aggregated, cotangent):
        preact = dot(aggregated, weight, 1, 0)
        sigmoid = jax.nn.sigmoid(preact)
        pre_grad = cotangent.astype(F32) * sigmoid * (1.0 + preact * (1.0 - sigmoid))
        return (preact * sigmoid).astype(BF16), pre_grad.astype(BF16)

    output_ref[...] = aggregates[0]
    _, own_grad = layer(aggregates[0], nodes[0][rows:, :])
    back_in = dot(own_grad, weight, 1, 1).astype(BF16)
    _, grads = layer(aggregated_ref[...], cotangent_ref[...])
    part = width // PAIR
    columns = aggregated_ref[:, :part]
    for half in range(1, PAIR):
        columns = jnp.where(core == half, aggregated_ref[:, half * part : (half + 1) * part], columns)
    grad = dot(columns, grads, 0, 0)
    asked = dot(wide_ref[...], grads, 1, 0).astype(BF16)
    back = dot(asked, weight, 1, 1).astype(BF16)
    for step in range(1, reps):
        term = dot(picked_ref[target_of("D", rep, step, reps)], back, 0, 0)
        sends[step - 1][...] = jnp.concatenate([term, grad], axis=0).astype(BF16)
    own = dot(picked_ref[rep], back, 0, 0) + back_in.astype(F32)
    kept_ref[...] = jnp.concatenate([own, grad], axis=0)


def output_kernel(aggregated_ref, weight_ref, output_ref):
    preact = dot(aggregated_ref[...], weight_ref[...], 1, 0)
    output_ref[...] = (preact * jax.nn.sigmoid(preact)).astype(BF16)


def layer_kernel(chips, slot_count, *refs):
    got, refs = refs[: PAIR * chips], refs[PAIR * chips :]
    features_ref, mate_features_ref, cotangent_ref, mate_cotangent_ref, weight_ref = refs[:5]
    output_ref, back_ref, *sends, grad_ref = refs[5:]
    rows, width = features_ref.shape
    wide = width // PAD
    core = lax.rem(lax.axis_index("rows"), PAIR)
    groups = pl.cdiv(PAIR * chips, wide)
    row = lax.broadcasted_iota(jnp.int32, (rows, width), 0)
    lane = lax.broadcasted_iota(jnp.int32, (rows, width), 1)
    valid = lax.rem(lane, PAD) < slot_count
    weight = weight_ref[...]
    hots, aggregates = [], []
    for half, own in ((core, features_ref), (1 - core, mate_features_ref)):
        first = pl.multiple_of(half * PAD, PAD)
        blocks = [ref[pl.ds(first, PAD), :] for ref in got]
        notes = [jnp.zeros((1, width), F32)] * groups
        for at, block in enumerate(blocks):
            mate = at // chips
            notes[at // wide] += block[16:].astype(F32)[slot_count - 16 + mate :][:1]
        parts = [
            jnp.where(valid & (note.astype(jnp.int32) == row), 1.0, 0.0).astype(BF16)
            for note in notes
        ]
        hot = parts[0] if groups == 1 else jnp.concatenate(parts, axis=1)
        hot = hot[:, : PAIR * chips * PAD]
        arrived = dot(hot, jnp.concatenate(blocks, axis=0), 1, 0)
        hots.append(hot[:, : chips * PAD])
        aggregates.append((own[...].astype(F32) + arrived).astype(BF16))
    aggregated = jnp.concatenate(aggregates, axis=0)
    preact = dot(aggregated, weight, 1, 0)
    sigmoid = jax.nn.sigmoid(preact)
    output_ref[...] = (preact * sigmoid)[:rows].astype(BF16)
    cotangent = jnp.concatenate([cotangent_ref[...], mate_cotangent_ref[...]], axis=0)
    pre_grad = (cotangent.astype(F32) * sigmoid * (1.0 + preact * (1.0 - sigmoid))).astype(BF16)
    back_in = dot(pre_grad, weight, 1, 1).astype(BF16)
    back_ref[...] = back_in[:rows]
    grad_ref[...] = dot(aggregated, pre_grad, 0, 0)
    part = width // PAIR
    grad = grad_ref[pl.ds(pl.multiple_of(core * part, part), part), :].astype(BF16)
    asked = [dot(hot, back_in[h * rows : (h + 1) * rows], 0, 0) for h, hot in enumerate(hots)]
    for step in range(chips):
        first = asked_at(step, chips) * PAD
        from_own, from_mate = (part[first : first + PAD].astype(BF16) for part in asked)
        sends[step][pl.ds(pl.multiple_of(core * PAD, PAD), PAD), :] = from_own
        sends[step][pl.ds(pl.multiple_of((1 - core) * PAD, PAD), PAD), :] = from_mate
        sends[step][PAIR * PAD :, :] = grad


def terms_kernel(reps, chips, picked_ref, back_ref, *refs):
    returned, kept_ref, sends = refs[:chips], refs[chips], refs[chips + 1 : -2]
    rows_ref, parts_ref = refs[-2:]
    rep = lax.axis_index("rep")
    chip = lax.div(lax.axis_index("rows"), PAIR)
    depth = PAIR * PAD
    for step in range(chips):
        origin = origin_of("C", chip, step, chips)
        rows_ref[pl.ds(pl.multiple_of(origin * depth, depth), depth), :] = returned[step][:depth, :]
        parts_ref[origin] = returned[step][depth:, :].astype(F32)
    part = parts_ref[0]
    for other in range(1, chips):
        part += parts_ref[other]
    rows = rows_ref[...]
    for step in range(1, reps):
        term = dot(picked_ref[target_of("D", rep, step, reps)], rows, 0, 0)
        sends[step - 1][...] = jnp.concatenate([term, part], axis=0).astype(BF16)
    own = dot(picked_ref[rep], rows, 0, 0) + back_ref[...].astype(F32)
    kept_ref[...] = jnp.concatenate([own, part], axis=0)


def chunk_kernel(reps, kept_ref, *refs):
    got, (chunk_ref, parts_ref) = refs[: reps - 1], refs[reps - 1 :]
    depth = chunk_ref.shape[0]
    rows = kept_ref.shape[0] - depth
    rep = lax.axis_index("rep")
    parts_ref[rep] = kept_ref[rows:, :].astype(BF16).astype(F32)
    for step in range(1, reps):
        parts_ref[origin_of("D", rep, step, reps)] = got[step - 1][rows:, :].astype(F32)
    chunk = parts_ref[0]
    for other in range(1, reps):
        chunk += parts_ref[other]
    chunk_ref[...] = chunk.astype(BF16)


def grad_x_kernel(kept_ref, *refs):
    got, grad_x_ref = refs[:-1], refs[-1]
    rows = grad_x_ref.shape[0]
    total = kept_ref[:rows, :]
    for ref in got:
        total += ref[:rows, :].astype(F32)
    grad_x_ref[...] = total.astype(BF16)


def grad_w_kernel(scale, own_ref, mate_ref, grad_w_ref):
    part = own_ref.shape[0]
    core = lax.rem(lax.axis_index("rows"), PAIR)
    for half, ref in ((core, own_ref), (1 - core, mate_ref)):
        first = pl.multiple_of(half * part, part)
        grad_w_ref[pl.ds(first, part), :] = ref[...].astype(F32) * scale


def local(features, weight, tiles, send_src, send_dst, cotangent):
    blocks = tiles[0, 0]
    source = send_src[0, 0]
    target = send_dst[0, 0]
    peers, slot_count = target.shape
    rows, width = features.shape
    cols, per_col, block = blocks.shape[:3]
    reps = lax.axis_size("rep")
    chips = peers // PAIR
    slots = peers * PAD
    chunk = width // PAIR
    plane = peers * slots <= MOST_ROWS

    def over_rep(name, value, step):
        return lax.ppermute(value, "rep", list(enumerate(targets(name, step, reps))))

    def over_chips(name, value, step):
        pairs = [
            (i * PAIR + core, to * PAIR + core)
            for i, to in enumerate(targets(name, step, chips))
            for core in range(PAIR)
        ]
        return lax.ppermute(value, "rows", pairs)

    def to_mate(value):
        return lax.ppermute(value, "rows", [(i, i ^ 1) for i in range(peers)])

    gathered = [over_rep("A", features, step) for step in range(1, reps)]

    picked, base, wanted = pl.pallas_call(
        lambda *refs: inputs_kernel(chips, plane, *refs),
        out_shape=(
            jax.ShapeDtypeStruct((cols, slots, block), BF16),
            jax.ShapeDtypeStruct((slots, width), F32),
            jax.ShapeDtypeStruct((slots, rows), BF16),
        ),
        in_specs=whole(4),
        out_specs=tuple(whole(3)),
        scratch_shapes=[
            pltpu.VMEM((peers, LANES), jnp.int32),
        ],
        compiler_params=params(slots),
        name="inputs",
    )(source, target, features, blocks)

    def partial(shape, count):
        return pl.pallas_call(
            lambda *refs: partial_kernel(reps, chips, *refs),
            out_shape=(jax.ShapeDtypeStruct(shape, BF16),) * count,
            in_specs=whole(1 + reps),
            out_specs=tuple(whole(count)),
            scratch_shapes=[pltpu.VMEM((slots, width), F32)],
            compiler_params=params(slots),
            name="partial",
        )(picked, base, *gathered)

    if plane:
        (outgoing,) = partial((slots, width), 1)
        both = jnp.concatenate([features, cotangent], axis=0)
        if chips == 4:
            low, high = (over_chips("B", both, step) for step in (2, 3))
            nodes = [both, over_chips("B", low, 3), low, high]
        else:
            nodes = [both] + [over_chips("B", both, step) for step in range(1, chips)]
        direct = [outgoing] + [over_chips("B", outgoing, step) for step in range(1, chips)]
        *late, _ = lax.optimization_barrier((*nodes, outgoing))
        hops = [to_mate(value) for value in late]
        if chips > 1:
            hops[0], hops[chips // 2], direct[1] = lax.optimization_barrier(
                (hops[0], hops[chips // 2], direct[1])
            )
        nodes += hops
        rows_in = direct + [to_mate(value) for value in direct]
        aggregated, kept, *sends = pl.pallas_call(
            lambda *refs: plane_kernel(reps, chips, slot_count, *refs),
            out_shape=(
                jax.ShapeDtypeStruct((rows, width), BF16),
                jax.ShapeDtypeStruct((rows + chunk, width), F32),
            )
            + (jax.ShapeDtypeStruct((rows + chunk, width), BF16),) * (reps - 1),
            in_specs=whole(3 + 2 * peers),
            out_specs=tuple(whole(1 + reps)),
            scratch_shapes=[
                pltpu.VMEM((peers * rows, width), BF16),
                pltpu.VMEM((peers * rows, width), BF16),
                pltpu.VMEM((peers, slots, width), BF16),
                pltpu.VMEM((slots, peers * rows), BF16),
            ],
            compiler_params=params(slots),
            name="plane",
        )(picked, wanted, weight, *rows_in, *nodes)
        output = pl.pallas_call(
            output_kernel,
            out_shape=jax.ShapeDtypeStruct((rows, width), BF16),
            in_specs=whole(2),
            out_specs=whole(1)[0],
            compiler_params=params(slots),
            name="output",
        )(aggregated, weight)
        kept, output = lax.optimization_barrier((kept, output))
    else:
        outgoing = partial((PAIR * PAD, width), chips)
        direct = [outgoing[0]] + [over_chips("B", outgoing[step], step) for step in range(1, chips)]
        shared = [to_mate(value) for value in direct]
        early_features, early_cotangent, _ = lax.optimization_barrier(
            (features, cotangent, outgoing[0])
        )

        output, back_in, *requested = pl.pallas_call(
            lambda *refs: layer_kernel(chips, slot_count, *refs),
            out_shape=(
                jax.ShapeDtypeStruct((rows, width), BF16),
                jax.ShapeDtypeStruct((rows, width), BF16),
            )
            + (jax.ShapeDtypeStruct((PAIR * PAD + chunk, width), BF16),) * chips,
            in_specs=whole(PAIR * chips + 5),
            out_specs=tuple(whole(2 + chips)),
            scratch_shapes=[pltpu.VMEM((width, width), F32)],
            compiler_params=params(slots),
            name="layer",
        )(
            *direct,
            *shared,
            features,
            to_mate(early_features),
            cotangent,
            to_mate(early_cotangent),
            weight,
        )

        returned = [requested[0]] + [over_chips("C", requested[step], step) for step in range(1, chips)]

        kept, *sends = pl.pallas_call(
            lambda *refs: terms_kernel(reps, chips, *refs),
            out_shape=(jax.ShapeDtypeStruct((rows + chunk, width), F32),)
            + (jax.ShapeDtypeStruct((rows + chunk, width), BF16),) * (reps - 1),
            in_specs=whole(2 + chips),
            out_specs=tuple(whole(reps)),
            scratch_shapes=[
                pltpu.VMEM((slots, width), BF16),
                pltpu.VMEM((chips, chunk, width), F32),
            ],
            compiler_params=params(slots),
            name="terms",
        )(picked, back_in, *returned)

    arrived = [over_rep("D", sends[step - 1], step) for step in range(1, reps)]

    share = pl.pallas_call(
        lambda *refs: chunk_kernel(reps, *refs),
        out_shape=jax.ShapeDtypeStruct((chunk, width), BF16),
        in_specs=whole(reps),
        out_specs=whole(1)[0],
        scratch_shapes=[pltpu.VMEM((reps, chunk, width), F32)],
        compiler_params=params(slots),
        name="chunk",
    )(kept, *arrived)

    grad_x = pl.pallas_call(
        grad_x_kernel,
        out_shape=jax.ShapeDtypeStruct((rows, width), BF16),
        in_specs=whole(reps),
        out_specs=whole(1)[0],
        compiler_params=params(slots),
        name="grad_x",
    )(kept, *arrived)

    node_count = rows * lax.axis_size("rows") * reps
    grad_w = pl.pallas_call(
        lambda *refs: grad_w_kernel(1.0 / math.sqrt(node_count), *refs),
        out_shape=jax.ShapeDtypeStruct((width, width), F32),
        in_specs=whole(2),
        out_specs=whole(1)[0],
        compiler_params=params(slots),
        name="grad_w",
    )(share, to_mate(share))
    return (output, grad_w, grad_x)


def solution(mesh):
    placed = (
        P(("rows", "rep"), None),
        P(),
        P("rows", "rep", None, None, None, None),
        P("rows", "rep", None, None),
        P("rows", "rep", None, None),
        P(("rows", "rep"), None),
    )
    return jax.shard_map(
        local,
        mesh=mesh,
        in_specs=placed,
        out_specs=(P(("rows", "rep"), None), P(), P(("rows", "rep"), None)),
        check_vma=False,
    )
```

```python
import math

import jax
import jax.numpy as jnp
from jax import lax
from jax.experimental import pallas as pl
from jax.experimental.pallas import tpu as pltpu
from jax.sharding import PartitionSpec as P

BF16 = jnp.bfloat16
F32 = jnp.float32
PAD = 32
LANES = 128
PAIR = 2
MOST_ROWS = 4096


def whole(count):
    return [pl.BlockSpec(memory_space=pltpu.VMEM)] * count


def params(slots):
    return pltpu.CompilerParams(vmem_limit_bytes=(4 << 20) + (16 << 10) * slots)


def dot(a, b, contract_a, contract_b):
    return lax.dot_general(
        a, b, (((contract_a,), (contract_b,)), ((), ())), preferred_element_type=F32
    )


LOW, HIGH, BOTH = (1, 0, 3, 2), (2, 3, 0, 1), (3, 2, 1, 0)
RING, REVERSE = (2, 3, 1, 0), (3, 2, 0, 1)
PLAN = dict(
    A=(LOW, BOTH, HIGH), B=(BOTH, LOW, HIGH), C=(LOW, HIGH, BOTH), D=(REVERSE, RING, LOW)
)


def targets(name, step, count):
    if step == 0:
        return tuple(range(count))
    if count == len(PLAN[name]) + 1:
        return PLAN[name][step - 1]
    return tuple((i + step) % count for i in range(count))


def entry(table, index):
    found = table[0]
    for i in range(1, len(table)):
        found = jnp.where(index == i, table[i], found)
    return found


def target_of(name, index, step, count):
    return entry(targets(name, step, count), index)


def origin_of(name, index, step, count):
    sent = targets(name, step, count)
    return entry(tuple(sent.index(i) for i in range(count)), index)


def step_to(name, index, other, count):
    found = jnp.zeros_like(other)
    for step in range(1, count):
        found = jnp.where(target_of(name, index, step, count) == other, step, found)
    return found


def asked_at(step, count):
    back = targets("C", step, count)
    for at in range(count):
        there = targets("B", at, count)
        if all(there[back[i]] == i for i in range(count)):
            return at
    raise ValueError("B and C differ")


def inputs_kernel(
    chips, plane, source_ref, target_ref, features_ref, tiles_ref, picked_ref, base_ref, wanted_ref, named_ref
):
    cols, per_col, block = tiles_ref.shape[:3]
    peers, slot_count = source_ref.shape
    slots, width = base_ref.shape
    wide = width // PAD
    chip = lax.div(lax.axis_index("rows"), PAIR)
    target = target_ref[...]
    named_ref[...] = jnp.full(named_ref.shape, -1, jnp.int32)
    named_ref[:, :slot_count] = jnp.where(target < features_ref.shape[0], source_ref[...], -1)
    spread = jnp.broadcast_to(named_ref[...][:, None, :], (peers, PAD, LANES)).reshape(slots, LANES)
    slot = lax.rem(lax.broadcasted_iota(jnp.int32, (slots, LANES), 0), PAD)
    lane = lax.broadcasted_iota(jnp.int32, (slots, LANES), 1)
    column = jnp.sum(jnp.where(lane == slot, spread, 0).astype(F32), axis=1, keepdims=True)
    offset = jnp.broadcast_to(column, (slots, LANES)) - lane.astype(F32)

    named_ref[...] = jnp.zeros(named_ref.shape, jnp.int32)
    named_ref[:, :slot_count] = target
    notes = named_ref[...]
    spread = jnp.broadcast_to(notes[:, None, :], (peers, PAD, LANES)).reshape(slots, LANES)
    landing = jnp.sum(jnp.where(lane == slot, spread, 0).astype(F32), axis=1, keepdims=True)
    here = (jnp.broadcast_to(landing, (slots, LANES)) == lane.astype(F32)) & (slot < slot_count)
    wanted_ref[...] = jnp.where(here, 1.0, 0.0).astype(BF16)
    tiled = notes
    for turn in range(1, LANES // PAD):
        tiled += pltpu.roll(notes, turn * PAD, 1)
    tiled = jnp.concatenate([tiled] * (width // LANES), axis=1)
    tiled = jnp.broadcast_to(tiled[:, None, :], (peers, PAD, width)).reshape(slots, width)
    row = lax.broadcasted_iota(jnp.int32, (slots, width), 0)
    if plane:
        keep = lax.rem(row, PAD) == slot_count
    else:
        spot = lax.div(lax.broadcasted_iota(jnp.int32, (slots, width), 1), PAD)
        at = step_to("B", chip, lax.div(row, PAD * PAIR), chips)
        keep = jnp.zeros((slots, width), jnp.bool_)
        for mate in range(PAIR):
            here = lax.rem(row, PAD) == slot_count + mate
            keep = keep | (here & (lax.rem(mate * chips + at, wide) == spot))
    landing = jnp.where(keep, tiled, 0).astype(F32)

    for b in range(cols):
        first = b * per_col
        hot = jnp.concatenate(
            [
                jnp.where(offset == float((first + k) * block), 1.0, 0.0).astype(BF16)
                for k in range(per_col)
            ],
            axis=1,
        )
        rows = tiles_ref[b].reshape(per_col * block, block)
        picked_ref[b] = dot(hot, rows, 1, 0).astype(BF16)
    base_ref[...] = landing + dot(picked_ref[lax.axis_index("rep")], features_ref[...], 1, 0)


def partial_kernel(reps, chips, picked_ref, base_ref, *refs):
    features, sends, total_ref = refs[: reps - 1], refs[reps - 1 : -1], refs[-1]
    rep = lax.axis_index("rep")
    chip = lax.div(lax.axis_index("rows"), PAIR)
    depth = PAIR * PAD
    total = base_ref[...]
    for step in range(1, reps):
        total += dot(picked_ref[origin_of("A", rep, step, reps)], features[step - 1][...], 1, 0)
    if len(sends) == 1:
        sends[0][...] = total.astype(BF16)
        return
    total_ref[...] = total
    for step in range(chips):
        first = pl.multiple_of(target_of("B", chip, step, chips) * depth, depth)
        sends[step][...] = total_ref[pl.ds(first, depth), :].astype(BF16)


def plane_kernel(reps, chips, slot_count, picked_ref, wanted_ref, weight_ref, *refs):
    peers = PAIR * chips
    got, nodes, refs = refs[:peers], refs[peers : 2 * peers], refs[2 * peers :]
    output_ref, kept_ref, *sends, aggregated_ref, cotangent_ref, block_ref, wide_ref = refs
    rows, width = output_ref.shape
    wide = width // PAD
    rep = lax.axis_index("rep")
    core = lax.rem(lax.axis_index("rows"), PAIR)
    chip = lax.div(lax.axis_index("rows"), PAIR)
    groups = pl.cdiv(peers, wide)
    wide_ref[...] = jnp.zeros(wide_ref.shape, BF16)
    for at in range(peers):
        here = slice(at * PAD, (at + 1) * PAD)
        wide_ref[here, at * rows : (at + 1) * rows] = wanted_ref[here, :]
    device = [
        origin_of("B", chip, at % chips, chips) * PAIR + (core if at < chips else 1 - core)
        for at in range(peers)
    ]
    row = lax.broadcasted_iota(jnp.int32, (rows, width), 0)
    lane = lax.broadcasted_iota(jnp.int32, (rows, width), 1)
    valid = lax.rem(lane, PAD) < slot_count
    spot = lax.div(lax.broadcasted_iota(jnp.int32, (1, width), 1), PAD)
    weight = weight_ref[...]
    hots = []
    for at in range(peers):
        first = pl.multiple_of(device[at] * PAD, PAD)
        notes = [jnp.zeros((1, width), F32)] * groups
        for source in range(peers):
            block = got[source][pl.ds(first, PAD), :]
            block_ref[at, pl.ds(pl.multiple_of(device[source] * PAD, PAD), PAD), :] = block
            note = block[16:].astype(F32)[slot_count - 16 :][:1]
            for e in range(groups):
                notes[e] = jnp.where(spot + e * wide == device[source], note, notes[e])
        parts = [
            jnp.where(valid & (note.astype(jnp.int32) == row), 1.0, 0.0).astype(BF16)
            for note in notes
        ]
        hot = parts[0] if groups == 1 else jnp.concatenate(parts, axis=1)
        hots.append(hot[:, : peers * PAD])
    arrived = [dot(hots[at], block_ref[at], 1, 0) for at in range(peers)]
    aggregates = [
        (nodes[at][:rows, :].astype(F32) + arrived[at]).astype(BF16) for at in range(peers)
    ]
    for at in range(peers):
        node = pl.multiple_of(device[at] * rows, rows)
        aggregated_ref[pl.ds(node, rows), :] = aggregates[at]
        cotangent_ref[pl.ds(node, rows), :] = nodes[at][rows:, :]

    def layer(aggregated, cotangent):
        preact = dot(aggregated, weight, 1, 0)
        sigmoid = jax.nn.sigmoid(preact)
        pre_grad = cotangent.astype(F32) * sigmoid * (1.0 + preact * (1.0 - sigmoid))
        return (preact * sigmoid).astype(BF16), pre_grad.astype(BF16)

    output_ref[...] = aggregates[0]
    _, grads = layer(aggregated_ref[...], cotangent_ref[...])
    part = width // PAIR
    columns = aggregated_ref[:, :part]
    for half in range(1, PAIR):
        columns = jnp.where(core == half, aggregated_ref[:, half * part : (half + 1) * part], columns)
    grad = dot(columns, grads, 0, 0)
    asked = dot(wide_ref[...], grads, 1, 0).astype(BF16)
    back = dot(asked, weight, 1, 1).astype(BF16)
    for step in range(1, reps):
        term = dot(picked_ref[target_of("D", rep, step, reps)], back, 0, 0)
        sends[step - 1][...] = jnp.concatenate([term, grad], axis=0).astype(BF16)
    own = dot(picked_ref[rep], back, 0, 0)
    kept_ref[...] = jnp.concatenate([own, grad], axis=0)


def output_kernel(aggregated_ref, cotangent_ref, weight_ref, output_ref, back_ref):
    weight = weight_ref[...]
    preact = dot(aggregated_ref[...], weight, 1, 0)
    sigmoid = jax.nn.sigmoid(preact)
    output_ref[...] = (preact * sigmoid).astype(BF16)
    pre_grad = cotangent_ref[...].astype(F32) * sigmoid * (1.0 + preact * (1.0 - sigmoid))
    back_ref[...] = dot(pre_grad.astype(BF16), weight, 1, 1).astype(BF16)


def layer_kernel(chips, slot_count, *refs):
    got, refs = refs[: PAIR * chips], refs[PAIR * chips :]
    features_ref, mate_features_ref, cotangent_ref, mate_cotangent_ref, weight_ref = refs[:5]
    output_ref, back_ref, *sends, grad_ref = refs[5:]
    rows, width = features_ref.shape
    wide = width // PAD
    core = lax.rem(lax.axis_index("rows"), PAIR)
    groups = pl.cdiv(PAIR * chips, wide)
    row = lax.broadcasted_iota(jnp.int32, (rows, width), 0)
    lane = lax.broadcasted_iota(jnp.int32, (rows, width), 1)
    valid = lax.rem(lane, PAD) < slot_count
    weight = weight_ref[...]
    hots, aggregates = [], []
    for half, own in ((core, features_ref), (1 - core, mate_features_ref)):
        first = pl.multiple_of(half * PAD, PAD)
        blocks = [ref[pl.ds(first, PAD), :] for ref in got]
        notes = [jnp.zeros((1, width), F32)] * groups
        for at, block in enumerate(blocks):
            mate = at // chips
            notes[at // wide] += block[16:].astype(F32)[slot_count - 16 + mate :][:1]
        parts = [
            jnp.where(valid & (note.astype(jnp.int32) == row), 1.0, 0.0).astype(BF16)
            for note in notes
        ]
        hot = parts[0] if groups == 1 else jnp.concatenate(parts, axis=1)
        hot = hot[:, : PAIR * chips * PAD]
        arrived = dot(hot, jnp.concatenate(blocks, axis=0), 1, 0)
        hots.append(hot[:, : chips * PAD])
        aggregates.append((own[...].astype(F32) + arrived).astype(BF16))
    aggregated = jnp.concatenate(aggregates, axis=0)
    preact = dot(aggregated, weight, 1, 0)
    sigmoid = jax.nn.sigmoid(preact)
    output_ref[...] = (preact * sigmoid)[:rows].astype(BF16)
    cotangent = jnp.concatenate([cotangent_ref[...], mate_cotangent_ref[...]], axis=0)
    pre_grad = (cotangent.astype(F32) * sigmoid * (1.0 + preact * (1.0 - sigmoid))).astype(BF16)
    back_in = dot(pre_grad, weight, 1, 1).astype(BF16)
    back_ref[...] = back_in[:rows]
    grad_ref[...] = dot(aggregated, pre_grad, 0, 0)
    part = width // PAIR
    grad = grad_ref[pl.ds(pl.multiple_of(core * part, part), part), :].astype(BF16)
    asked = [dot(hot, back_in[h * rows : (h + 1) * rows], 0, 0) for h, hot in enumerate(hots)]
    for step in range(chips):
        first = asked_at(step, chips) * PAD
        from_own, from_mate = (part[first : first + PAD].astype(BF16) for part in asked)
        sends[step][pl.ds(pl.multiple_of(core * PAD, PAD), PAD), :] = from_own
        sends[step][pl.ds(pl.multiple_of((1 - core) * PAD, PAD), PAD), :] = from_mate
        sends[step][PAIR * PAD :, :] = grad


def terms_kernel(reps, chips, picked_ref, back_ref, *refs):
    returned, kept_ref, sends = refs[:chips], refs[chips], refs[chips + 1 : -2]
    rows_ref, parts_ref = refs[-2:]
    rep = lax.axis_index("rep")
    chip = lax.div(lax.axis_index("rows"), PAIR)
    depth = PAIR * PAD
    for step in range(chips):
        origin = origin_of("C", chip, step, chips)
        rows_ref[pl.ds(pl.multiple_of(origin * depth, depth), depth), :] = returned[step][:depth, :]
        parts_ref[origin] = returned[step][depth:, :].astype(F32)
    part = parts_ref[0]
    for other in range(1, chips):
        part += parts_ref[other]
    rows = rows_ref[...]
    for step in range(1, reps):
        term = dot(picked_ref[target_of("D", rep, step, reps)], rows, 0, 0)
        sends[step - 1][...] = jnp.concatenate([term, part], axis=0).astype(BF16)
    own = dot(picked_ref[rep], rows, 0, 0) + back_ref[...].astype(F32)
    kept_ref[...] = jnp.concatenate([own, part], axis=0)


def chunk_kernel(reps, kept_ref, *refs):
    got, (chunk_ref, parts_ref) = refs[: reps - 1], refs[reps - 1 :]
    depth = chunk_ref.shape[0]
    rows = kept_ref.shape[0] - depth
    rep = lax.axis_index("rep")
    parts_ref[rep] = kept_ref[rows:, :].astype(BF16).astype(F32)
    for step in range(1, reps):
        parts_ref[origin_of("D", rep, step, reps)] = got[step - 1][rows:, :].astype(F32)
    chunk = parts_ref[0]
    for other in range(1, reps):
        chunk += parts_ref[other]
    chunk_ref[...] = chunk.astype(BF16)


def grad_x_kernel(kept_ref, *refs):
    got, grad_x_ref = refs[:-1], refs[-1]
    rows = grad_x_ref.shape[0]
    total = kept_ref[:rows, :]
    for ref in got:
        total += ref[:rows, :].astype(F32)
    grad_x_ref[...] = total.astype(BF16)


def grad_w_kernel(scale, own_ref, mate_ref, grad_w_ref):
    part = own_ref.shape[0]
    core = lax.rem(lax.axis_index("rows"), PAIR)
    for half, ref in ((core, own_ref), (1 - core, mate_ref)):
        first = pl.multiple_of(half * part, part)
        grad_w_ref[pl.ds(first, part), :] = ref[...].astype(F32) * scale


def local(features, weight, tiles, send_src, send_dst, cotangent):
    blocks = tiles[0, 0]
    source = send_src[0, 0]
    target = send_dst[0, 0]
    peers, slot_count = target.shape
    rows, width = features.shape
    cols, per_col, block = blocks.shape[:3]
    reps = lax.axis_size("rep")
    chips = peers // PAIR
    slots = peers * PAD
    chunk = width // PAIR
    plane = peers * slots <= MOST_ROWS

    def over_rep(name, value, step):
        return lax.ppermute(value, "rep", list(enumerate(targets(name, step, reps))))

    def over_chips(name, value, step):
        pairs = [
            (i * PAIR + core, to * PAIR + core)
            for i, to in enumerate(targets(name, step, chips))
            for core in range(PAIR)
        ]
        return lax.ppermute(value, "rows", pairs)

    def to_mate(value):
        return lax.ppermute(value, "rows", [(i, i ^ 1) for i in range(peers)])

    gathered = [over_rep("A", features, step) for step in range(1, reps)]

    picked, base, wanted = pl.pallas_call(
        lambda *refs: inputs_kernel(chips, plane, *refs),
        out_shape=(
            jax.ShapeDtypeStruct((cols, slots, block), BF16),
            jax.ShapeDtypeStruct((slots, width), F32),
            jax.ShapeDtypeStruct((slots, rows), BF16),
        ),
        in_specs=whole(4),
        out_specs=tuple(whole(3)),
        scratch_shapes=[
            pltpu.VMEM((peers, LANES), jnp.int32),
        ],
        compiler_params=params(slots),
        name="inputs",
    )(source, target, features, blocks)

    def partial(shape, count):
        return pl.pallas_call(
            lambda *refs: partial_kernel(reps, chips, *refs),
            out_shape=(jax.ShapeDtypeStruct(shape, BF16),) * count,
            in_specs=whole(1 + reps),
            out_specs=tuple(whole(count)),
            scratch_shapes=[pltpu.VMEM((slots, width), F32)],
            compiler_params=params(slots),
            name="partial",
        )(picked, base, *gathered)

    if plane:
        (outgoing,) = partial((slots, width), 1)
        both = jnp.concatenate([features, cotangent], axis=0)
        if chips == 4:
            low, high = (over_chips("B", both, step) for step in (2, 3))
            nodes = [both, over_chips("B", low, 3), low, high]
        else:
            nodes = [both] + [over_chips("B", both, step) for step in range(1, chips)]
        direct = [outgoing] + [over_chips("B", outgoing, step) for step in range(1, chips)]
        *late, _ = lax.optimization_barrier((*nodes, outgoing))
        hops = [to_mate(value) for value in late]
        if chips > 1:
            hops[0], hops[chips // 2], direct[1] = lax.optimization_barrier(
                (hops[0], hops[chips // 2], direct[1])
            )
        nodes += hops
        rows_in = direct + [to_mate(value) for value in direct]
        aggregated, kept, *sends = pl.pallas_call(
            lambda *refs: plane_kernel(reps, chips, slot_count, *refs),
            out_shape=(
                jax.ShapeDtypeStruct((rows, width), BF16),
                jax.ShapeDtypeStruct((rows + chunk, width), F32),
            )
            + (jax.ShapeDtypeStruct((rows + chunk, width), BF16),) * (reps - 1),
            in_specs=whole(3 + 2 * peers),
            out_specs=tuple(whole(1 + reps)),
            scratch_shapes=[
                pltpu.VMEM((peers * rows, width), BF16),
                pltpu.VMEM((peers * rows, width), BF16),
                pltpu.VMEM((peers, slots, width), BF16),
                pltpu.VMEM((slots, peers * rows), BF16),
            ],
            compiler_params=params(slots),
            name="plane",
        )(picked, wanted, weight, *rows_in, *nodes)
        output, back_in = pl.pallas_call(
            output_kernel,
            out_shape=(jax.ShapeDtypeStruct((rows, width), BF16),) * 2,
            in_specs=whole(3),
            out_specs=tuple(whole(2)),
            compiler_params=params(slots),
            name="output",
        )(aggregated, cotangent, weight)
        kept, output, back_in = lax.optimization_barrier((kept, output, back_in))
        backs = [back_in]
    else:
        backs = []
        outgoing = partial((PAIR * PAD, width), chips)
        direct = [outgoing[0]] + [over_chips("B", outgoing[step], step) for step in range(1, chips)]
        shared = [to_mate(value) for value in direct]
        early_features, early_cotangent, _ = lax.optimization_barrier(
            (features, cotangent, outgoing[0])
        )

        output, back_in, *requested = pl.pallas_call(
            lambda *refs: layer_kernel(chips, slot_count, *refs),
            out_shape=(
                jax.ShapeDtypeStruct((rows, width), BF16),
                jax.ShapeDtypeStruct((rows, width), BF16),
            )
            + (jax.ShapeDtypeStruct((PAIR * PAD + chunk, width), BF16),) * chips,
            in_specs=whole(PAIR * chips + 5),
            out_specs=tuple(whole(2 + chips)),
            scratch_shapes=[pltpu.VMEM((width, width), F32)],
            compiler_params=params(slots),
            name="layer",
        )(
            *direct,
            *shared,
            features,
            to_mate(early_features),
            cotangent,
            to_mate(early_cotangent),
            weight,
        )

        returned = [requested[0]] + [over_chips("C", requested[step], step) for step in range(1, chips)]

        kept, *sends = pl.pallas_call(
            lambda *refs: terms_kernel(reps, chips, *refs),
            out_shape=(jax.ShapeDtypeStruct((rows + chunk, width), F32),)
            + (jax.ShapeDtypeStruct((rows + chunk, width), BF16),) * (reps - 1),
            in_specs=whole(2 + chips),
            out_specs=tuple(whole(reps)),
            scratch_shapes=[
                pltpu.VMEM((slots, width), BF16),
                pltpu.VMEM((chips, chunk, width), F32),
            ],
            compiler_params=params(slots),
            name="terms",
        )(picked, back_in, *returned)

    arrived = [over_rep("D", sends[step - 1], step) for step in range(1, reps)]

    share = pl.pallas_call(
        lambda *refs: chunk_kernel(reps, *refs),
        out_shape=jax.ShapeDtypeStruct((chunk, width), BF16),
        in_specs=whole(reps),
        out_specs=whole(1)[0],
        scratch_shapes=[pltpu.VMEM((reps, chunk, width), F32)],
        compiler_params=params(slots),
        name="chunk",
    )(kept, *arrived)

    grad_x = pl.pallas_call(
        grad_x_kernel,
        out_shape=jax.ShapeDtypeStruct((rows, width), BF16),
        in_specs=whole(reps + len(backs)),
        out_specs=whole(1)[0],
        compiler_params=params(slots),
        name="grad_x",
    )(kept, *backs, *arrived)

    node_count = rows * lax.axis_size("rows") * reps
    grad_w = pl.pallas_call(
        lambda *refs: grad_w_kernel(1.0 / math.sqrt(node_count), *refs),
        out_shape=jax.ShapeDtypeStruct((width, width), F32),
        in_specs=whole(2),
        out_specs=whole(1)[0],
        compiler_params=params(slots),
        name="grad_w",
    )(share, to_mate(share))
    return (output, grad_w, grad_x)


def solution(mesh):
    placed = (
        P(("rows", "rep"), None),
        P(),
        P("rows", "rep", None, None, None, None),
        P("rows", "rep", None, None),
        P("rows", "rep", None, None),
        P(("rows", "rep"), None),
    )
    return jax.shard_map(
        local,
        mesh=mesh,
        in_specs=placed,
        out_specs=(P(("rows", "rep"), None), P(), P(("rows", "rep"), None)),
        check_vma=False,
    )
```
